32 devices in a mesh: parts: 2 (over y), ffn: 4 (over z), pair: 2 (over x), rep: 2 (over core).
Axes of the slice: x: 2, y: 2, z: 4, core: 2. Of those that a mesh axis runs over, the one named last changes fastest.
Arguments:
- residual: float32 [2, 8, 16, 8192], P(None, ('parts', 'pair', 'rep'), 'ffn'), parts along dimension 1, may hold values from -6 to 6
- query: bfloat16 [2, 8, 16, 8192], P(None, ('parts', 'pair', 'rep'), 'ffn'), parts along dimension 1, may hold values from -6 to 6
- key_cache: bfloat16 [2, 8, 16, 128, 1024], P(None, ('parts', 'pair', 'rep'), 'ffn'), parts along dimension 1, may hold values from -6 to 6
- value_cache: bfloat16 [2, 8, 16, 128, 1024], P(None, ('parts', 'pair', 'rep'), 'ffn'), parts along dimension 1, may hold values from -6 to 6
- cache_len: int32 [2, 8, 16], P(None, ('parts', 'pair', 'rep'), 'ffn'), parts along dimension 1, may hold values from 32 to 128, as said below
- partner_table: int32 [4, 4], P('parts'), parts along dimension 0, may hold values from 0 to 3, each once within a row
- norm_gain: float32 [8192], replicated, may hold values from 0.1 to 1.9
- gate_weight: bfloat16 [8192, 14336], P(('pair', 'rep'), 'ffn'), may hold values from -0.0625 to 0.0625
- up_weight: bfloat16 [8192, 14336], P(('pair', 'rep'), 'ffn'), may hold values from -0.0625 to 0.0625
- down_weight: bfloat16 [14336, 8192], P('ffn', ('pair', 'rep')), may hold values from -0.046875 to 0.046875
Outputs:
- new_residual: float32 [2, 8, 16, 8192], P(None, ('parts', 'pair', 'rep'), 'ffn'), parts along dimension 1
- served_hidden: bfloat16 [2, 8, 16, 14336], P(None, ('parts', 'pair', 'rep'), None, 'ffn'), parts along dimension 1
The draws below stay inside these ranges and needn't reach their ends.
There are 2 independent parts, one for each index of `parts`. The reference program is written for one: setup_inputs(seed, part) draws one part's arguments, and reference() takes and returns one part's arrays. A program takes and returns all parts, laid end to end along the dimension named above; an argument that names none is the same for every part. Nothing has to cross between parts.
Inputs may be any that keep to these rules, and one draw needn't show every extreme that they name: `cache_len`: one entry of each sequence's new token; some sequence has exactly 128. `partner_table`: each row names every column once.
All inputs are finite; a program needn't handle non-finite values.
Results may differ from the reference program's by a relative error of at most 0.0085.
Values may be sent and summed in bfloat16 or wider, within the bound.
No kernel may reach another device: no remote copies, remote signals or barrier semaphores. Data moves between devices by JAX's collectives and lax.ppermute only.
A program may use at most 128 MiB of HBM per device.

```python
import math
import jax
import jax.numpy as jnp
from jax import lax

D = 8192
FF = 14336
HEADS = 64
KVH = 8
HD = 128
MB = 2
CACHE = 128
NG = 4
ROWS_G = 16


def draw_query(key, part):
    key = jax.random.fold_in(key, 11)
    shape = (MB, NG, ROWS_G, HEADS * HD)
    base = jnp.clip(jax.random.normal(key, shape), -5.5, 5.5)
    return base.astype(jnp.bfloat16)


def draw_key_cache(key, part):
    key = jax.random.fold_in(key, 23)
    shape = (MB, NG, ROWS_G, CACHE, KVH * HD)
    base = jnp.clip(jax.random.normal(key, shape), -5.5, 5.5)
    return base.astype(jnp.bfloat16)


def draw_cache_len(key, part):
    key = jax.random.fold_in(key, 37)
    first_key, second_key = jax.random.split(key)
    shape = (MB, NG, ROWS_G)
    lengths = jax.random.randint(first_key, shape, max(2, CACHE // 4), CACHE + 1)
    target = jax.random.randint(second_key, (), 0, MB * NG * ROWS_G)
    flat_index = jnp.arange(MB * NG * ROWS_G).reshape(shape)
    return jnp.where(flat_index == target, CACHE, lengths).astype(jnp.int32)


def shard_levels(stream_key, shape, cuts, low, top_value):
    def one(dim, blocks):
        heights = jax.random.uniform(jax.random.fold_in(jax.random.fold_in(stream_key, 6), dim), (blocks,), jnp.float32, low / len(cuts), top_value / len(cuts))
        return jnp.repeat(jnp.exp(heights), shape[dim] // blocks).reshape((-1,) + (1,) * (len(shape) - dim - 1))

    loudness = one(*cuts[0])
    for cut in cuts[1:]:
        loudness = loudness * one(*cut)
    return loudness


def bell_draw(key, extent, deviation, most, cuts=(), dtype=jnp.bfloat16):
    array = jax.random.normal(key, extent, jnp.float32) * deviation
    if len(cuts) > 0:
        array = shard_levels(key, extent, cuts, -0.22, 0.18) * array
    return jnp.clip(array, min=-most, max=most).astype(dtype)


def setup_inputs(seed: int = 0, part: int = 0) -> dict:
    key_list = jax.random.split(jax.random.key(seed), 11)
    own_keys = jax.random.split(jax.random.fold_in(key_list[10], part), 11)
    return {
        "residual": bell_draw(own_keys[0], (MB, NG, ROWS_G, D), 1.0, 6.0, ((1, 4), (2, 4)), jnp.float32),
        "query": draw_query(jax.random.fold_in(jax.random.fold_in(key_list[10], part), 71), part),
        "key_cache": draw_key_cache(jax.random.fold_in(jax.random.fold_in(key_list[10], part), 71), part),
        "value_cache": bell_draw(own_keys[3], (MB, NG, ROWS_G, CACHE, KVH * HD), 1.0, 6.0, ((1, 4), (2, 4))),
        "cache_len": draw_cache_len(jax.random.fold_in(jax.random.fold_in(key_list[10], part), 71), part),
        "partner_table": jax.vmap(lambda own: jax.random.permutation(own, NG))(jax.random.split(own_keys[5], MB)).reshape((MB, NG)).astype(jnp.int32),
        "norm_gain": jnp.clip(1.0 + 0.18 * jax.random.normal(key_list[6], (D,), jnp.float32), 0.1, 1.9),
        "gate_weight": bell_draw(key_list[7], (D, FF), D ** -0.5, 0.0625, ((0, 4), (1, 4))),
        "up_weight": bell_draw(key_list[8], (D, FF), D ** -0.5, 0.0625, ((0, 4), (1, 4))),
        "down_weight": bell_draw(key_list[9], (FF, D), FF ** -0.5, 0.046875, ((0, 4), (1, 4))),
    }


def attend(query, key_cache, value_cache, cache_len):
    rows = query.shape[0]
    scale = 1.0 / math.sqrt(HD)
    queries = query.astype(jnp.float32).reshape(rows, KVH, HEADS // KVH, HD)
    keys = key_cache.astype(jnp.float32).reshape(rows, CACHE, KVH, HD)
    values = value_cache.astype(jnp.float32).reshape(rows, CACHE, KVH, HD)
    scores = jnp.einsum('rkgd,rlkd->rkgl', queries, keys) * scale
    valid = (jnp.arange(CACHE)[None, :] < cache_len[:, None])[:, None, None, :]
    scores = jnp.where(valid, scores, -1e+30)
    peak = lax.optimization_barrier(jnp.max(scores, axis=-1, keepdims=True))
    raised = jnp.exp(scores - peak)
    attn_probs = (raised / lax.optimization_barrier(jnp.sum(raised, axis=-1, keepdims=True))).astype(jnp.bfloat16)
    mixed = jnp.einsum('rkgl,rlkd->rkgd', attn_probs.astype(jnp.float32), values)
    return mixed.astype(jnp.bfloat16).reshape(rows, HEADS * HD)

def reference(residual, query, key_cache, value_cache, cache_len, partner_table, norm_gain, gate_weight, up_weight, down_weight):
    flat_query = query.reshape(MB * NG, ROWS_G, HEADS * HD)
    flat_keys = key_cache.reshape(MB * NG, ROWS_G, CACHE, KVH * HD)
    flat_values = value_cache.reshape(MB * NG, ROWS_G, CACHE, KVH * HD)
    flat_len = cache_len.reshape(MB * NG, ROWS_G)
    attn = lax.map(lambda item: attend(item[0], item[1], item[2], item[3]), (flat_query, flat_keys, flat_values, flat_len))
    attn = attn.reshape(MB, NG, ROWS_G, D)
    stream = residual + attn.astype(jnp.float32)
    normed = (stream * lax.rsqrt(lax.optimization_barrier(jnp.mean(stream * stream, axis=-1, keepdims=True)) + 1e-05) * norm_gain).astype(jnp.bfloat16)
    flat_rows = normed.reshape(MB * NG * ROWS_G, D)
    gate = jnp.dot(flat_rows, gate_weight, preferred_element_type=jnp.float32)
    upper = jnp.dot(flat_rows, up_weight, preferred_element_type=jnp.float32)
    hidden = (jax.nn.silu(gate) * upper).astype(jnp.bfloat16)
    change = jnp.dot(hidden, down_weight, preferred_element_type=jnp.float32).astype(jnp.bfloat16)
    new_residual = stream + change.reshape(MB, NG, ROWS_G, D).astype(jnp.float32)
    hidden_full = hidden.reshape(MB, NG, ROWS_G, FF)
    chosen = (partner_table[:, :, None] == jnp.arange(NG)[None, None, :]).astype(jnp.float32)
    served_hidden = jnp.einsum('mac,marf->mcrf', chosen, hidden_full.astype(jnp.float32)).astype(jnp.bfloat16)
    return (new_residual, served_hidden)
```

```python
import functools
import math

import jax
import jax.numpy as jnp
from jax import lax
from jax.experimental import pallas as pl
from jax.experimental.pallas import tpu as pltpu
from jax.sharding import PartitionSpec as P

HD = 128
F32 = jnp.float32
BF16 = jnp.bfloat16
SMEM = pltpu.MemorySpace.SMEM
VMEM = pltpu.MemorySpace.VMEM


def attend_kernel(
    cols, kvh, heads_per_step, len_ref, query_ref, key_ref, value_ref, residual_ref, gain_ref, *refs
):
    pairs, reps = cols
    stream_ref = refs[0]
    piece_refs = refs[1 : 1 + pairs * reps]
    bias_ref, = refs[1 + pairs * reps :]
    step = pl.program_id(0)
    batches, rows, wide = query_ref.shape
    seqs = batches * rows
    cache = key_ref.shape[0] // seqs
    group = wide // (heads_per_step * HD)
    scale = 1.0 / math.sqrt(HD)

    @pl.when(step == 0)
    def _():
        shape = (group * seqs, seqs * cache)
        row = lax.rem(lax.broadcasted_iota(jnp.int32, shape, 0), seqs)
        place = lax.broadcasted_iota(jnp.int32, shape, 1) - row * cache
        limit = jnp.zeros(shape, jnp.int32)
        for seq in range(seqs):
            limit = jnp.where(row == seq, len_ref[seq // rows, seq % rows], limit)
        bias_ref[...] = jnp.where((place >= 0) & (place < limit), 0.0, -1e30)

    queries = jnp.concatenate([query_ref[b].astype(F32) for b in range(batches)], axis=0)
    residual = jnp.concatenate([residual_ref[b] for b in range(batches)], axis=0)
    mixed = []
    for k in range(heads_per_step):
        stacked = jnp.concatenate(
            [queries[:, (k * group + h) * HD : (k * group + h + 1) * HD] for h in range(group)],
            axis=0,
        ).astype(BF16)
        scores = lax.dot_general(
            stacked,
            key_ref[:, k * HD : (k + 1) * HD],
            (((1,), (1,)), ((), ())),
            preferred_element_type=F32,
        )
        scores = scores * scale + bias_ref[...]
        peak = jnp.max(scores, axis=-1, keepdims=True)
        raised = jnp.exp(scores - peak)
        probs = (raised / jnp.sum(raised, axis=-1, keepdims=True)).astype(BF16)
        out = jnp.dot(probs, value_ref[:, k * HD : (k + 1) * HD], preferred_element_type=F32)
        out = out.astype(BF16).astype(F32)
        mixed += [out[h * seqs : (h + 1) * seqs] for h in range(group)]
    start = pl.multiple_of(step * wide, wide)
    stream_ref[:, pl.ds(start, wide)] = residual + jnp.concatenate(mixed, axis=1)

    @pl.when(step == kvh // heads_per_step - 1)
    def _():
        stream = stream_ref[...]
        width = stream.shape[1] // (pairs * reps)
        factor = lax.rsqrt(jnp.mean(stream * stream, axis=-1, keepdims=True) + 1e-05)
        pair = lax.axis_index("pair")
        rep = lax.axis_index("rep")
        for index, piece_ref in enumerate(piece_refs):
            dr, dp = divmod(index, pairs)
            column = lax.rem(pair + dp, pairs) * reps + lax.rem(rep + dr, reps)
            own = pl.ds(pl.multiple_of(column * width, width), width)
            piece_ref[...] = (stream_ref[:, own] * factor * gain_ref[:, own]).astype(BF16)


def attend(cols, cache_len, query, key_cache, value_cache, residual, norm_gain):
    batches, _, rows, depth = query.shape
    seqs = batches * rows
    cache, kv = key_cache.shape[3:]
    kvh = kv // HD
    heads_per_step = 2
    wide = depth // kvh * heads_per_step
    columns = cols[0] * cols[1]
    by_head = pl.BlockSpec((batches, rows, wide), lambda i: (0, 0, i))
    cached = pl.BlockSpec((seqs * cache, heads_per_step * HD), lambda i: (0, i))
    return pl.pallas_call(
        functools.partial(attend_kernel, cols, kvh, heads_per_step),
        grid=(kvh // heads_per_step,),
        out_shape=[jax.ShapeDtypeStruct((seqs, depth), F32)]
        + [jax.ShapeDtypeStruct((seqs, depth // columns), BF16)] * columns,
        in_specs=[
            pl.BlockSpec(memory_space=SMEM),
            by_head,
            cached,
            cached,
            by_head,
            pl.BlockSpec((1, depth), lambda i: (0, 0)),
        ],
        out_specs=[pl.BlockSpec((seqs, depth), lambda i: (0, 0))]
        + [pl.BlockSpec((seqs, depth // columns), lambda i: (0, 0))] * columns,
        scratch_shapes=[pltpu.VMEM((depth // kvh // HD * seqs, seqs * cache), F32)],
        compiler_params=pltpu.CompilerParams(vmem_limit_bytes=16 * 1024 * 1024),
        cost_estimate=pl.CostEstimate(flops=10**9, bytes_accessed=10**7, transcendentals=10**6),
        name="attend",
    )(
        cache_len.reshape(batches, rows),
        query.reshape(batches, rows, depth),
        key_cache.reshape(seqs * cache, kv),
        value_cache.reshape(seqs * cache, kv),
        residual.reshape(batches, rows, depth),
        norm_gain.reshape(1, depth),
    )


def owner_of(table_ref, micro, column, columns):
    found = jnp.int32(0)
    for group in range(columns):
        found = found + jnp.where(table_ref[micro, group] == column, group, 0)
    return found


def gate_up_kernel(cols, batches, ffn, table_ref, *refs):
    pairs, reps = cols
    columns = pairs * reps
    pieces = refs[:ffn]
    gate_ref, up_ref, keep_ref, send_ref, rows_ref = refs[ffn:]
    seqs = pieces[0].shape[1]
    rows = seqs // batches
    half = rows_ref.shape[0] // reps

    @pl.when(pl.program_id(0) == 0)
    def _():
        pair = lax.axis_index("pair")
        rep = lax.axis_index("rep")
        first = lax.broadcasted_iota(jnp.int32, pieces[0].shape[1:], 0) < rows
        for index in range(columns):
            dr, dp = divmod(index, pairs)
            column = lax.rem(pair + dp, pairs) * reps + lax.rem(rep + dr, reps)
            for micro in range(batches):
                group = owner_of(table_ref, micro, column, columns)
                from_pair = lax.rem(pair - group // reps + pairs, pairs)
                from_rep = lax.rem(rep - lax.rem(group, reps) + reps, reps)
                slot = from_rep * pairs + from_pair
                for shift in range(0, ffn, 2):
                    a = pieces[shift][slot].astype(F32)
                    b = pieces[shift + 1][slot].astype(F32)
                    if micro == 0:
                        b = pltpu.roll(b, rows, 0)
                    else:
                        a = pltpu.roll(a, rows, 0)
                    base = ((index * batches + micro) * ffn + shift) * rows
                    rows_ref[base : base + 2 * rows, :] = jnp.where(first, a, b).astype(BF16)

    for place, weight_ref in enumerate((gate_ref, up_ref)):
        sums = jnp.dot(rows_ref[...], weight_ref[...], preferred_element_type=F32)
        keep_ref[place] = sums[:half]
        send_ref[place] = sums[half:].astype(BF16)


def gate_up(cols, batches, table, pieces, gate_weight, up_weight, chunk, chunks):
    ffn = len(pieces)
    columns, seqs, depth = pieces[0].shape
    width = gate_weight.shape[1] // chunks
    tile = math.gcd(width, 256)
    steps = width // tile
    total = columns * seqs * ffn
    half = total // cols[1]
    weight = pl.BlockSpec((depth, tile), lambda i: (0, chunk * steps + i))
    whole = pl.BlockSpec((columns, seqs, depth), lambda i: (0, 0, 0))
    out = pl.BlockSpec((2, half, tile), lambda i: (0, 0, i))
    return pl.pallas_call(
        functools.partial(gate_up_kernel, cols, batches, ffn),
        grid=(steps,),
        out_shape=[
            jax.ShapeDtypeStruct((2, half, width), F32),
            jax.ShapeDtypeStruct((2, total - half, width), BF16),
        ],
        in_specs=[pl.BlockSpec(memory_space=SMEM)] + [whole] * ffn + [weight, weight],
        out_specs=[out, pl.BlockSpec((2, total - half, tile), lambda i: (0, 0, i))],
        scratch_shapes=[pltpu.VMEM((total, depth), BF16)],
        compiler_params=pltpu.CompilerParams(vmem_limit_bytes=32 * 1024 * 1024),
        cost_estimate=pl.CostEstimate(
            flops=4 * total * depth * width, bytes_accessed=4 * depth * width, transcendentals=0
        ),
        name=f"gate_up_{chunk}",
    )(table, *pieces, gate_weight, up_weight)


def join_kernel(pairs, keep_ref, came_ref, own_ref, *send_refs):
    rows = own_ref.shape[1]
    own_ref[...] = keep_ref[:, :rows] + came_ref[:, :rows].astype(F32)
    for dp in range(1, pairs):
        part = slice(dp * rows, (dp + 1) * rows)
        send_refs[dp - 1][...] = (keep_ref[:, part] + came_ref[:, part].astype(F32)).astype(BF16)


def join(pairs, keep, came):
    two, total, width = keep.shape
    rows = total // pairs
    tile = math.gcd(width, 896)

    def block(count):
        return pl.BlockSpec((two, count, tile), lambda i: (0, 0, i))

    return pl.pallas_call(
        functools.partial(join_kernel, pairs),
        grid=(width // tile,),
        out_shape=[jax.ShapeDtypeStruct((two, rows, width), F32)]
        + [jax.ShapeDtypeStruct((two, rows, width), BF16)] * (pairs - 1),
        in_specs=[block(total)] * 2,
        out_specs=[block(rows)] * pairs,
        compiler_params=pltpu.CompilerParams(vmem_limit_bytes=16 * 1024 * 1024),
        cost_estimate=pl.CostEstimate(flops=keep.size, bytes_accessed=6 * keep.size, transcendentals=0),
        name="join",
    )(keep, came)


def act_kernel(own_ref, *refs):
    sums = own_ref[...]
    for ref in refs[:-1]:
        sums = sums + ref[...].astype(F32)
    gate = sums[0]
    refs[-1][...] = (gate / (1.0 + jnp.exp(-gate)) * sums[1]).astype(BF16)


def activate(own, arrived):
    two, rows, width = own.shape
    tile = math.gcd(width, 896)
    block = pl.BlockSpec((two, rows, tile), lambda i: (0, 0, i))
    return pl.pallas_call(
        act_kernel,
        grid=(width // tile,),
        out_shape=jax.ShapeDtypeStruct((rows, width), BF16),
        in_specs=[block] * (1 + len(arrived)),
        out_specs=pl.BlockSpec((rows, tile), lambda i: (0, i)),
        compiler_params=pltpu.CompilerParams(vmem_limit_bytes=16 * 1024 * 1024),
        cost_estimate=pl.CostEstimate(flops=own.size, bytes_accessed=6 * own.size, transcendentals=own.size),
        name="activate",
    )(own, *arrived)


def served_kernel(batches, rows, *refs):
    out_ref = refs[-1]
    turn = lax.axis_index("ffn") * rows
    start = 0
    for ref in refs[:-1]:
        held = ref[...].astype(F32)
        each = held.shape[0] // batches
        for micro in range(batches):
            part = pltpu.roll(held[micro * each : (micro + 1) * each], turn, 0)
            out_ref[micro, 0, :, start : start + held.shape[1]] = part.astype(BF16)
        start += held.shape[1]


def serve(batches, rows, hidden):
    total = hidden[0].shape[0]
    width = sum(h.shape[1] for h in hidden)
    return pl.pallas_call(
        functools.partial(served_kernel, batches, rows),
        out_shape=jax.ShapeDtypeStruct((batches, 1, total // batches, width), BF16),
        in_specs=[pl.BlockSpec(memory_space=VMEM)] * len(hidden),
        out_specs=pl.BlockSpec(memory_space=VMEM),
        compiler_params=pltpu.CompilerParams(vmem_limit_bytes=16 * 1024 * 1024),
        name="serve",
    )(*hidden)


def down_kernel(count, has_sum, hidden_count, *refs):
    hidden_refs = refs[:hidden_count]
    weight_ref = refs[hidden_count]
    out_ref = refs[-2]
    rows_ref = refs[-1]

    @pl.when(pl.program_id(0) == 0)
    def _():
        rows_ref[...] = jnp.concatenate([ref[...] for ref in hidden_refs], axis=0)

    sums = jnp.dot(rows_ref[...], weight_ref[...], preferred_element_type=F32)
    if has_sum:
        sums = sums + refs[hidden_count + 1][...]
    out_ref[...] = sums


def down(hidden, weight, chunk, chunks, before):
    width = weight.shape[0] // chunks
    depth = weight.shape[1]
    tile = math.gcd(depth, 256)
    total = sum(h.shape[0] for h in hidden)
    part = pl.BlockSpec((total, tile), lambda i: (0, i))
    return pl.pallas_call(
        functools.partial(down_kernel, chunks, before is not None, len(hidden)),
        grid=(depth // tile,),
        out_shape=jax.ShapeDtypeStruct((total, depth), F32),
        in_specs=[pl.BlockSpec(h.shape, lambda i: (0, 0)) for h in hidden]
        + [pl.BlockSpec((width, tile), lambda i: (chunk, i))]
        + [part] * (before is not None),
        out_specs=part,
        scratch_shapes=[pltpu.VMEM((total, width), BF16)],
        compiler_params=pltpu.CompilerParams(vmem_limit_bytes=32 * 1024 * 1024),
        cost_estimate=pl.CostEstimate(
            flops=2 * total * depth * width, bytes_accessed=2 * depth * width, transcendentals=0
        ),
        name=f"down_{chunk}",
    )(*hidden, weight, *([before] * (before is not None)))


def arrange_kernel(cols, batches, ffn, rows, table_ref, sums_ref, *out_refs):
    pairs, reps = cols
    columns = pairs * reps
    pair = lax.axis_index("pair")
    rep = lax.axis_index("rep")
    seqs = batches * rows
    first = lax.broadcasted_iota(jnp.int32, (seqs, sums_ref.shape[1]), 0) < rows
    for index in range(columns):
        dr, dp = divmod(index, pairs)
        group = lax.rem(pair + dp, pairs) * reps + lax.rem(rep + dr, reps)
        bases = []
        for micro in range(batches):
            column = table_ref[micro, group]
            to_pair = lax.rem(column // reps - pair + pairs, pairs)
            to_rep = lax.rem(lax.rem(column, reps) - rep + reps, reps)
            bases.append(((to_rep * pairs + to_pair) * batches + micro) * ffn * rows)
        for shift in range(ffn):
            low = shift // 2 * 2 * rows
            a, b = (
                sums_ref[pl.ds(pl.multiple_of(base + low, 2 * rows), 2 * rows), :] for base in bases
            )
            if shift % 2 == 0:
                b = pltpu.roll(b, rows, 0)
            else:
                a = pltpu.roll(a, rows, 0)
            out_refs[shift][index] = jnp.where(first, a, b).astype(BF16)


def arrange(cols, batches, ffn, rows, table, sums):
    columns = cols[0] * cols[1]
    depth = sums.shape[1]
    return pl.pallas_call(
        functools.partial(arrange_kernel, cols, batches, ffn, rows),
        out_shape=[jax.ShapeDtypeStruct((columns, batches * rows, depth), BF16)] * ffn,
        in_specs=[pl.BlockSpec(memory_space=SMEM), pl.BlockSpec(memory_space=VMEM)],
        out_specs=[pl.BlockSpec(memory_space=VMEM)] * ffn,
        compiler_params=pltpu.CompilerParams(vmem_limit_bytes=16 * 1024 * 1024),
        name="arrange",
    )(table, sums)


def total_kernel(*refs):
    count = len(refs) // 2
    ins = [r for r in refs if r.ndim == 3]
    outs = [r for r in refs if r.ndim == 2]
    for index, out_ref in enumerate(outs):
        sums = ins[0][index].astype(F32)
        for ref in ins[1:]:
            sums = sums + ref[index].astype(F32)
        out_ref[...] = sums.astype(BF16)


def total(parts):
    columns, seqs, depth = parts[0].shape
    return pl.pallas_call(
        total_kernel,
        out_shape=[jax.ShapeDtypeStruct((seqs, depth), BF16)] * columns,
        in_specs=[pl.BlockSpec(memory_space=VMEM)] * len(parts),
        out_specs=[pl.BlockSpec(memory_space=VMEM)] * columns,
        compiler_params=pltpu.CompilerParams(vmem_limit_bytes=16 * 1024 * 1024),
        name="total",
    )(*parts)


def finish_kernel(cols, stream_ref, *refs):
    pairs, reps = cols
    pair = lax.axis_index("pair")
    rep = lax.axis_index("rep")
    out_ref = refs[-1]
    batches, _, rows, _ = out_ref.shape
    width = refs[0].shape[1]
    for index, ref in enumerate(refs[:-1]):
        dr, dp = divmod(index, pairs)
        column = lax.rem(pair - dp + pairs, pairs) * reps + lax.rem(rep - dr + reps, reps)
        own = pl.ds(pl.multiple_of(column * width, width), width)
        sums = stream_ref[:, own] + ref[...].astype(F32)
        for micro in range(batches):
            out_ref[micro, 0, :, own] = sums[micro * rows : (micro + 1) * rows]


def finish(cols, batches, stream, changes):
    seqs, depth = stream.shape
    return pl.pallas_call(
        functools.partial(finish_kernel, cols),
        out_shape=jax.ShapeDtypeStruct((batches, 1, seqs // batches, depth), F32),
        in_specs=[pl.BlockSpec(memory_space=VMEM)] * (1 + len(changes)),
        out_specs=pl.BlockSpec(memory_space=VMEM),
        compiler_params=pltpu.CompilerParams(vmem_limit_bytes=16 * 1024 * 1024),
        name="finish",
    )(stream, *changes)


def to_column(cols, value, dr, dp):
    pairs, reps = cols
    route = [
        (p * reps + r, (p + dp) % pairs * reps + (r + dr) % reps)
        for p in range(pairs)
        for r in range(reps)
    ]
    return lax.ppermute(value, ("pair", "rep"), route)


def exchange(cols, values):
    return [values[0]] + [
        to_column(cols, value, *divmod(index, cols[0]))
        for index, value in enumerate(values)
        if index > 0
    ]


def per_device(
    cols,
    ffn,
    residual,
    query,
    key_cache,
    value_cache,
    cache_len,
    partner_table,
    norm_gain,
    gate_weight,
    up_weight,
    down_weight,
):
    pairs, reps = cols
    batches, _, rows, _ = query.shape
    units = gate_weight.shape[1] // 128
    chunks = 2 if units % 2 == 0 else 1
    stream, *normed = attend(
        cols, cache_len, query, key_cache, value_cache, residual, norm_gain
    )
    mine = jnp.stack(exchange(cols, normed))
    pieces = [mine] + [
        lax.ppermute(mine, "ffn", [(i, (i - s) % ffn) for i in range(ffn)]) for s in range(1, ffn)
    ]
    hidden = []
    sums = None
    for chunk in range(chunks):
        keep, send = gate_up(
            cols, batches, partner_table, pieces, gate_weight, up_weight, chunk, chunks
        )
        came = to_column(cols, send, 1, 0)
        own, *others = join(pairs, keep, came)
        arrived = [to_column(cols, other, 0, dp + 1) for dp, other in enumerate(others)]
        hidden.append(activate(own, arrived))
    for chunk, part in enumerate(hidden):
        block = [part] + [to_column(cols, part, 0, pairs - dp) for dp in range(1, pairs)]
        block += [to_column(cols, item, 1, 0) for item in block]
        sums = down(block, down_weight, chunk, chunks, sums)
    served = serve(batches, rows, hidden)
    shares = arrange(cols, batches, ffn, rows, partner_table, sums)
    gathered = [shares[0]] + [
        lax.ppermute(shares[s], "ffn", [(i, (i + s) % ffn) for i in range(ffn)])
        for s in range(1, ffn)
    ]
    changes = exchange(cols, total(gathered))
    updated = finish(cols, batches, stream, changes)
    return (updated, served)


def solution(mesh):
    sizes = dict(mesh.shape)
    cols = (sizes["pair"], sizes["rep"])
    rows = P(None, ("parts", "pair", "rep"), "ffn", None)
    caches = P(None, ("parts", "pair", "rep"), "ffn", None, None)
    placed = (
        rows,
        rows,
        caches,
        caches,
        P(None, ("parts", "pair", "rep"), "ffn"),
        P("parts", None),
        P(),
        P(("pair", "rep"), "ffn"),
        P(("pair", "rep"), "ffn"),
        P("ffn", ("pair", "rep")),
    )
    return jax.shard_map(
        functools.partial(per_device, cols, sizes["ffn"]),
        mesh=mesh,
        in_specs=placed,
        out_specs=(rows, P(None, ("parts", "pair", "rep"), None, "ffn")),
        check_vma=False,
    )
```

```python
import functools
import math

import jax
import jax.numpy as jnp
from jax import lax
from jax.experimental import pallas as pl
from jax.experimental.pallas import tpu as pltpu
from jax.sharding import PartitionSpec as P

HD = 128
F32 = jnp.float32
BF16 = jnp.bfloat16
SMEM = pltpu.MemorySpace.SMEM
VMEM = pltpu.MemorySpace.VMEM


def in_hbm(value):
    return pltpu.with_memory_space_constraint(value, pltpu.MemorySpace.HBM)


def attend_kernel(
    cols, kvh, heads_per_step, len_ref, query_ref, key_ref, value_ref, residual_ref, gain_ref, *refs
):
    pairs, reps = cols
    stream_ref = refs[0]
    piece_refs = refs[1 : 1 + pairs * reps]
    bias_ref, = refs[1 + pairs * reps :]
    step = pl.program_id(0)
    batches, rows, wide = query_ref.shape
    seqs = batches * rows
    cache = key_ref.shape[0] // seqs
    group = wide // (heads_per_step * HD)
    scale = 1.0 / math.sqrt(HD)

    @pl.when(step == 0)
    def _():
        shape = (group * seqs, seqs * cache)
        row = lax.rem(lax.broadcasted_iota(jnp.int32, shape, 0), seqs)
        place = lax.broadcasted_iota(jnp.int32, shape, 1) - row * cache
        limit = jnp.zeros(shape, jnp.int32)
        for seq in range(seqs):
            limit = jnp.where(row == seq, len_ref[seq // rows, seq % rows], limit)
        bias_ref[...] = jnp.where((place >= 0) & (place < limit), 0.0, -1e30)

    queries = jnp.concatenate([query_ref[b].astype(F32) for b in range(batches)], axis=0)
    residual = jnp.concatenate([residual_ref[b] for b in range(batches)], axis=0)
    mixed = []
    for k in range(heads_per_step):
        stacked = jnp.concatenate(
            [queries[:, (k * group + h) * HD : (k * group + h + 1) * HD] for h in range(group)],
            axis=0,
        ).astype(BF16)
        scores = lax.dot_general(
            stacked,
            key_ref[:, k * HD : (k + 1) * HD],
            (((1,), (1,)), ((), ())),
            preferred_element_type=F32,
        )
        scores = scores * scale + bias_ref[...]
        peak = jnp.max(scores, axis=-1, keepdims=True)
        raised = jnp.exp(scores - peak)
        probs = (raised / jnp.sum(raised, axis=-1, keepdims=True)).astype(BF16)
        out = jnp.dot(probs, value_ref[:, k * HD : (k + 1) * HD], preferred_element_type=F32)
        out = out.astype(BF16).astype(F32)
        mixed += [out[h * seqs : (h + 1) * seqs] for h in range(group)]
    start = pl.multiple_of(step * wide, wide)
    stream_ref[:, pl.ds(start, wide)] = residual + jnp.concatenate(mixed, axis=1)

    @pl.when(step == kvh // heads_per_step - 1)
    def _():
        stream = stream_ref[...]
        width = stream.shape[1] // (pairs * reps)
        factor = lax.rsqrt(jnp.mean(stream * stream, axis=-1, keepdims=True) + 1e-05)
        pair = lax.axis_index("pair")
        rep = lax.axis_index("rep")
        for index, piece_ref in enumerate(piece_refs):
            dr, dp = divmod(index, pairs)
            column = lax.rem(pair + dp, pairs) * reps + lax.rem(rep + dr, reps)
            own = pl.ds(pl.multiple_of(column * width, width), width)
            piece_ref[...] = (stream_ref[:, own] * factor * gain_ref[:, own]).astype(BF16)


def attend(cols, cache_len, query, key_cache, value_cache, residual, norm_gain):
    batches, _, rows, depth = query.shape
    seqs = batches * rows
    cache, kv = key_cache.shape[3:]
    kvh = kv // HD
    heads_per_step = 2
    wide = depth // kvh * heads_per_step
    columns = cols[0] * cols[1]
    by_head = pl.BlockSpec((batches, rows, wide), lambda i: (0, 0, i))
    cached = pl.BlockSpec((seqs * cache, heads_per_step * HD), lambda i: (0, i))
    return pl.pallas_call(
        functools.partial(attend_kernel, cols, kvh, heads_per_step),
        grid=(kvh // heads_per_step,),
        out_shape=[jax.ShapeDtypeStruct((seqs, depth), F32)]
        + [jax.ShapeDtypeStruct((seqs, depth // columns), BF16)] * columns,
        in_specs=[
            pl.BlockSpec(memory_space=SMEM),
            by_head,
            cached,
            cached,
            by_head,
            pl.BlockSpec((1, depth), lambda i: (0, 0)),
        ],
        out_specs=[pl.BlockSpec((seqs, depth), lambda i: (0, 0))]
        + [pl.BlockSpec((seqs, depth // columns), lambda i: (0, 0))] * columns,
        scratch_shapes=[pltpu.VMEM((depth // kvh // HD * seqs, seqs * cache), F32)],
        compiler_params=pltpu.CompilerParams(vmem_limit_bytes=8 * 1024 * 1024),
        cost_estimate=pl.CostEstimate(flops=10**11, bytes_accessed=10**8, transcendentals=10**8),
        name="attend",
    )(
        cache_len.reshape(batches, rows),
        in_hbm(query.reshape(batches, rows, depth)),
        in_hbm(key_cache.reshape(seqs * cache, kv)),
        in_hbm(value_cache.reshape(seqs * cache, kv)),
        in_hbm(residual.reshape(batches, rows, depth)),
        in_hbm(norm_gain.reshape(1, depth)),
    )


def owner_of(table_ref, micro, column, columns):
    found = jnp.int32(0)
    for group in range(columns):
        found = found + jnp.where(table_ref[micro, group] == column, group, 0)
    return found


def gate_up_kernel(cols, batches, ffn, start, table_ref, *refs):
    pairs, reps = cols
    columns = pairs * reps
    pieces = refs[:ffn]
    gate_ref, up_ref, keep_ref, send_ref, rows_ref = refs[ffn:]
    seqs = pieces[0].shape[1]
    rows = seqs // batches
    half = rows_ref.shape[0] // reps

    def order():
        pair = lax.axis_index("pair")
        rep = lax.axis_index("rep")
        first = lax.broadcasted_iota(jnp.int32, pieces[0].shape[1:], 0) < rows
        for index in range(columns):
            dr, dp = divmod(index, pairs)
            column = lax.rem(pair + dp, pairs) * reps + lax.rem(rep + dr, reps)
            for micro in range(batches):
                group = owner_of(table_ref, micro, column, columns)
                from_pair = lax.rem(pair - group // reps + pairs, pairs)
                from_rep = lax.rem(rep - lax.rem(group, reps) + reps, reps)
                slot = from_rep * pairs + from_pair
                for shift in range(0, ffn, 2):
                    a = pieces[shift][slot].astype(F32)
                    b = pieces[shift + 1][slot].astype(F32)
                    if micro == 0:
                        b = pltpu.roll(b, rows, 0)
                    else:
                        a = pltpu.roll(a, rows, 0)
                    base = ((index * batches + micro) * ffn + shift) * rows
                    rows_ref[base : base + 2 * rows, :] = jnp.where(first, a, b).astype(BF16)

    order()
    width = keep_ref.shape[2]
    tile = math.gcd(width, 256)
    for place, weight_ref in enumerate((gate_ref, up_ref)):
        for low in range(0, width, tile):
            part = slice(low, low + tile)
            sums = jnp.dot(
                rows_ref[...],
                weight_ref[:, start + low : start + low + tile],
                preferred_element_type=F32,
            )
            keep_ref[place, :, part] = sums[:half]
            send_ref[place, :, part] = sums[half:].astype(BF16)


def gate_up(cols, batches, table, pieces, gate_weight, up_weight, chunk, chunks):
    ffn = len(pieces)
    columns, seqs, depth = pieces[0].shape
    width = gate_weight.shape[1] // chunks
    total = columns * seqs * ffn
    half = total // cols[1]
    whole = pl.BlockSpec(memory_space=VMEM)
    return pl.pallas_call(
        functools.partial(gate_up_kernel, cols, batches, ffn, chunk * width),
        out_shape=[
            jax.ShapeDtypeStruct((2, half, width), F32),
            jax.ShapeDtypeStruct((2, total - half, width), BF16),
        ],
        in_specs=[pl.BlockSpec(memory_space=SMEM)] + [whole] * (ffn + 2),
        out_specs=[whole, whole],
        scratch_shapes=[pltpu.VMEM((total, depth), BF16)],
        compiler_params=pltpu.CompilerParams(vmem_limit_bytes=8 * 1024 * 1024),
        cost_estimate=pl.CostEstimate(
            flops=10**11, bytes_accessed=10**8, transcendentals=0
        ),
        name=f"gate_up_{chunk}",
    )(table, *pieces, gate_weight, up_weight)


def join_kernel(pairs, keep_ref, came_ref, own_ref, *send_refs):
    rows = own_ref.shape[1]
    own_ref[...] = keep_ref[:, :rows] + came_ref[:, :rows].astype(F32)
    for dp in range(1, pairs):
        part = slice(dp * rows, (dp + 1) * rows)
        send_refs[dp - 1][...] = (keep_ref[:, part] + came_ref[:, part].astype(F32)).astype(BF16)


def join(pairs, keep, came):
    two, total, width = keep.shape
    rows = total // pairs
    tile = math.gcd(width, 896)

    def block(count):
        return pl.BlockSpec((two, count, tile), lambda i: (0, 0, i))

    return pl.pallas_call(
        functools.partial(join_kernel, pairs),
        grid=(width // tile,),
        out_shape=[jax.ShapeDtypeStruct((two, rows, width), F32)]
        + [jax.ShapeDtypeStruct((two, rows, width), BF16)] * (pairs - 1),
        in_specs=[block(total)] * 2,
        out_specs=[block(rows)] * pairs,
        compiler_params=pltpu.CompilerParams(vmem_limit_bytes=8 * 1024 * 1024),
        cost_estimate=pl.CostEstimate(flops=keep.size, bytes_accessed=6 * keep.size, transcendentals=0),
        name="join",
    )(keep, came)


def act_kernel(own_ref, *refs):
    sums = own_ref[...]
    for ref in refs[:-1]:
        sums = sums + ref[...].astype(F32)
    gate = sums[0]
    refs[-1][...] = (gate / (1.0 + jnp.exp(-gate)) * sums[1]).astype(BF16)


def activate(own, arrived):
    two, rows, width = own.shape
    tile = math.gcd(width, 896)
    block = pl.BlockSpec((two, rows, tile), lambda i: (0, 0, i))
    return pl.pallas_call(
        act_kernel,
        grid=(width // tile,),
        out_shape=jax.ShapeDtypeStruct((rows, width), BF16),
        in_specs=[block] * (1 + len(arrived)),
        out_specs=pl.BlockSpec((rows, tile), lambda i: (0, i)),
        compiler_params=pltpu.CompilerParams(vmem_limit_bytes=8 * 1024 * 1024),
        cost_estimate=pl.CostEstimate(flops=own.size, bytes_accessed=6 * own.size, transcendentals=own.size),
        name="activate",
    )(own, *arrived)


def served_kernel(batches, rows, *refs):
    out_ref = refs[-1]
    turn = lax.axis_index("ffn") * rows
    start = 0
    for ref in refs[:-1]:
        held = ref[...].astype(F32)
        each = held.shape[0] // batches
        for micro in range(batches):
            part = pltpu.roll(held[micro * each : (micro + 1) * each], turn, 0)
            out_ref[micro, 0, :, start : start + held.shape[1]] = part.astype(BF16)
        start += held.shape[1]


def serve(batches, rows, hidden):
    total = hidden[0].shape[0]
    width = sum(h.shape[1] for h in hidden)
    return pl.pallas_call(
        functools.partial(served_kernel, batches, rows),
        out_shape=jax.ShapeDtypeStruct((batches, 1, total // batches, width), BF16),
        in_specs=[pl.BlockSpec(memory_space=VMEM)] * len(hidden),
        out_specs=pl.BlockSpec(memory_space=VMEM),
        compiler_params=pltpu.CompilerParams(vmem_limit_bytes=8 * 1024 * 1024),
        name="serve",
    )(*hidden)


def down_kernel(start, has_sum, hidden_count, *refs):
    hidden_refs = refs[:hidden_count]
    weight_ref = refs[hidden_count]
    out_ref = refs[-1]
    rows = jnp.concatenate([ref[...] for ref in hidden_refs], axis=0)
    depth = out_ref.shape[1]
    tile = math.gcd(depth, 256)
    for low in range(0, depth, tile):
        part = slice(low, low + tile)
        sums = jnp.dot(
            rows, weight_ref[start : start + rows.shape[1], part], preferred_element_type=F32
        )
        if has_sum:
            sums = sums + refs[hidden_count + 1][:, part]
        out_ref[:, part] = sums


def down(hidden, weight, chunk, chunks, before):
    width = weight.shape[0] // chunks
    depth = weight.shape[1]
    total = sum(h.shape[0] for h in hidden)
    whole = pl.BlockSpec(memory_space=VMEM)
    return pl.pallas_call(
        functools.partial(down_kernel, chunk * width, before is not None, len(hidden)),
        out_shape=jax.ShapeDtypeStruct((total, depth), F32),
        in_specs=[whole] * (len(hidden) + 1 + (before is not None)),
        out_specs=whole,
        compiler_params=pltpu.CompilerParams(vmem_limit_bytes=8 * 1024 * 1024),
        cost_estimate=pl.CostEstimate(
            flops=2 * total * depth * width, bytes_accessed=2 * depth * width, transcendentals=0
        ),
        name=f"down_{chunk}",
    )(*hidden, weight, *([before] * (before is not None)))


def arrange_kernel(cols, batches, ffn, rows, table_ref, sums_ref, *out_refs):
    pairs, reps = cols
    columns = pairs * reps
    pair = lax.axis_index("pair")
    rep = lax.axis_index("rep")
    seqs = batches * rows
    first = lax.broadcasted_iota(jnp.int32, (seqs, sums_ref.shape[1]), 0) < rows
    for index in range(columns):
        dr, dp = divmod(index, pairs)
        group = lax.rem(pair + dp, pairs) * reps + lax.rem(rep + dr, reps)
        bases = []
        for micro in range(batches):
            column = table_ref[micro, group]
            to_pair = lax.rem(column // reps - pair + pairs, pairs)
            to_rep = lax.rem(lax.rem(column, reps) - rep + reps, reps)
            bases.append(((to_rep * pairs + to_pair) * batches + micro) * ffn * rows)
        for shift in range(ffn):
            low = shift // 2 * 2 * rows
            a, b = (
                sums_ref[pl.ds(pl.multiple_of(base + low, 2 * rows), 2 * rows), :] for base in bases
            )
            if shift % 2 == 0:
                b = pltpu.roll(b, rows, 0)
            else:
                a = pltpu.roll(a, rows, 0)
            out_refs[shift][index] = jnp.where(first, a, b).astype(BF16)


def arrange(cols, batches, ffn, rows, table, sums):
    columns = cols[0] * cols[1]
    depth = sums.shape[1]
    return pl.pallas_call(
        functools.partial(arrange_kernel, cols, batches, ffn, rows),
        out_shape=[jax.ShapeDtypeStruct((columns, batches * rows, depth), BF16)] * ffn,
        in_specs=[pl.BlockSpec(memory_space=SMEM), pl.BlockSpec(memory_space=VMEM)],
        out_specs=[pl.BlockSpec(memory_space=VMEM)] * ffn,
        compiler_params=pltpu.CompilerParams(vmem_limit_bytes=8 * 1024 * 1024),
        name="arrange",
    )(table, sums)


def total_kernel(*refs):
    count = len(refs) // 2
    ins = [r for r in refs if r.ndim == 3]
    outs = [r for r in refs if r.ndim == 2]
    for index, out_ref in enumerate(outs):
        sums = ins[0][index].astype(F32)
        for ref in ins[1:]:
            sums = sums + ref[index].astype(F32)
        out_ref[...] = sums.astype(BF16)


def total(parts):
    columns, seqs, depth = parts[0].shape
    return pl.pallas_call(
        total_kernel,
        out_shape=[jax.ShapeDtypeStruct((seqs, depth), BF16)] * columns,
        in_specs=[pl.BlockSpec(memory_space=VMEM)] * len(parts),
        out_specs=[pl.BlockSpec(memory_space=VMEM)] * columns,
        compiler_params=pltpu.CompilerParams(vmem_limit_bytes=8 * 1024 * 1024),
        name="total",
    )(*parts)


def finish_kernel(cols, stream_ref, *refs):
    pairs, reps = cols
    pair = lax.axis_index("pair")
    rep = lax.axis_index("rep")
    out_ref = refs[-1]
    batches, _, rows, _ = out_ref.shape
    width = refs[0].shape[1]
    for index, ref in enumerate(refs[:-1]):
        dr, dp = divmod(index, pairs)
        column = lax.rem(pair - dp + pairs, pairs) * reps + lax.rem(rep - dr + reps, reps)
        own = pl.ds(pl.multiple_of(column * width, width), width)
        sums = stream_ref[:, own] + ref[...].astype(F32)
        for micro in range(batches):
            out_ref[micro, 0, :, own] = sums[micro * rows : (micro + 1) * rows]


def finish(cols, batches, stream, changes):
    seqs, depth = stream.shape
    return pl.pallas_call(
        functools.partial(finish_kernel, cols),
        out_shape=jax.ShapeDtypeStruct((batches, 1, seqs // batches, depth), F32),
        in_specs=[pl.BlockSpec(memory_space=VMEM)] * (1 + len(changes)),
        out_specs=pl.BlockSpec(memory_space=VMEM),
        compiler_params=pltpu.CompilerParams(vmem_limit_bytes=8 * 1024 * 1024),
        name="finish",
    )(stream, *changes)


def to_column(cols, value, dr, dp):
    pairs, reps = cols
    route = [
        (p * reps + r, (p + dp) % pairs * reps + (r + dr) % reps)
        for p in range(pairs)
        for r in range(reps)
    ]
    return lax.ppermute(value, ("pair", "rep"), route)


def exchange(cols, values):
    return [values[0]] + [
        to_column(cols, value, *divmod(index, cols[0]))
        for index, value in enumerate(values)
        if index > 0
    ]


def per_device(
    cols,
    ffn,
    residual,
    query,
    key_cache,
    value_cache,
    cache_len,
    partner_table,
    norm_gain,
    gate_weight,
    up_weight,
    down_weight,
):
    pairs, reps = cols
    batches, _, rows, _ = query.shape
    units = gate_weight.shape[1] // 128
    chunks = 2 if units % 2 == 0 else 1
    stream, *normed = attend(
        cols, cache_len, query, key_cache, value_cache, residual, norm_gain
    )
    mine = jnp.stack(exchange(cols, normed))
    pieces = [mine] + [
        lax.ppermute(mine, "ffn", [(i, (i - s) % ffn) for i in range(ffn)]) for s in range(1, ffn)
    ]
    hidden = []
    sums = None
    for chunk in range(chunks):
        keep, send = gate_up(
            cols, batches, partner_table, pieces, gate_weight, up_weight, chunk, chunks
        )
        came = to_column(cols, send, 1, 0)
        own, *others = join(pairs, keep, came)
        arrived = [to_column(cols, other, 0, dp + 1) for dp, other in enumerate(others)]
        hidden.append(activate(own, arrived))
    for chunk, part in enumerate(hidden):
        block = [part] + [to_column(cols, part, 0, pairs - dp) for dp in range(1, pairs)]
        block += [to_column(cols, item, 1, 0) for item in block]
        sums = down(block, down_weight, chunk, chunks, sums)
    served = serve(batches, rows, hidden)
    shares = arrange(cols, batches, ffn, rows, partner_table, sums)
    gathered = [shares[0]] + [
        lax.ppermute(shares[s], "ffn", [(i, (i + s) % ffn) for i in range(ffn)])
        for s in range(1, ffn)
    ]
    changes = exchange(cols, total(gathered))
    updated = finish(cols, batches, stream, changes)
    return (updated, served)


def solution(mesh):
    sizes = dict(mesh.shape)
    cols = (sizes["pair"], sizes["rep"])
    rows = P(None, ("parts", "pair", "rep"), "ffn", None)
    caches = P(None, ("parts", "pair", "rep"), "ffn", None, None)
    placed = (
        rows,
        rows,
        caches,
        caches,
        P(None, ("parts", "pair", "rep"), "ffn"),
        P("parts", None),
        P(),
        P(("pair", "rep"), "ffn"),
        P(("pair", "rep"), "ffn"),
        P("ffn", ("pair", "rep")),
    )
    return jax.shard_map(
        functools.partial(per_device, cols, sizes["ffn"]),
        mesh=mesh,
        in_specs=placed,
        out_specs=(rows, P(None, ("parts", "pair", "rep"), None, "ffn")),
        check_vma=False,
    )
```

```python
import functools
import math

import jax
import jax.numpy as jnp
from jax import lax
from jax.experimental import pallas as pl
from jax.experimental.pallas import tpu as pltpu
from jax.sharding import PartitionSpec as P

HD = 128
F32 = jnp.float32
BF16 = jnp.bfloat16
SMEM = pltpu.MemorySpace.SMEM
VMEM = pltpu.MemorySpace.VMEM
WHOLE = pl.BlockSpec(memory_space=VMEM)
UNREAD = pl.BlockSpec(memory_space=pl.ANY)
LONG = 5 * 10**10
TABLE = pl.BlockSpec(memory_space=SMEM)


def in_hbm(value):
    return pltpu.with_memory_space_constraint(value, pltpu.MemorySpace.HBM)


def params(size=4):
    return pltpu.CompilerParams(vmem_limit_bytes=size * 1024 * 1024)


def cost(flops=10**6):
    return pl.CostEstimate(flops=flops, bytes_accessed=flops // 1000, transcendentals=0)


def place_of(index, cols, sign=1):
    pairs, reps = cols
    dr, dp = divmod(index, pairs)
    pair = lax.rem(lax.axis_index("pair") + sign * dp + pairs, pairs)
    rep = lax.rem(lax.axis_index("rep") + sign * dr + reps, reps)
    return pair * reps + rep


def attend_kernel(
    cols, kvh, per_step, len_ref, query_ref, key_ref, value_ref, residual_ref, gain_ref, *refs
):
    pairs, reps = cols
    stream_ref = refs[0]
    piece_refs = refs[1 : 1 + pairs * reps]
    bias_ref, = refs[1 + pairs * reps :]
    step = pl.program_id(0)
    batches, rows, wide = query_ref.shape
    seqs = batches * rows
    cache = key_ref.shape[0] // seqs
    group = wide // (per_step * HD)
    each = group * seqs
    scale = 1.0 / math.sqrt(HD)

    @pl.when(step == 0)
    def _():
        seq = lax.rem(lax.broadcasted_iota(jnp.int32, bias_ref.shape, 1), seqs)
        place = lax.broadcasted_iota(jnp.int32, bias_ref.shape, 0)
        limit = jnp.zeros(bias_ref.shape, jnp.int32)
        for one in range(seqs):
            limit = jnp.where(seq == one, len_ref[one // rows, one % rows], limit)
        bias_ref[...] = jnp.where(place < limit, 0.0, -1e30)

    queries = jnp.concatenate([query_ref[b].astype(F32) for b in range(batches)], axis=0)
    residual = jnp.concatenate([residual_ref[b] for b in range(batches)], axis=0)
    lane_seq = lax.rem(lax.broadcasted_iota(jnp.int32, (cache, 2 * each), 1), seqs)
    row_seq = lax.rem(lax.broadcasted_iota(jnp.int32, (2 * each, cache), 0), seqs)
    mixed = []
    for low in range(0, per_step, 2):
        both = slice(low * HD, (low + 2) * HD)
        blocks = []
        for k in range(2):
            heads = range((low + k) * group, (low + k + 1) * group)
            stacked = jnp.concatenate([queries[:, h * HD : (h + 1) * HD] for h in heads], axis=0)
            empty = jnp.zeros_like(stacked)
            blocks.append(jnp.concatenate([empty, stacked] if k else [stacked, empty], axis=1))
        spread = jnp.concatenate(blocks, axis=0).astype(BF16)
        scores = None
        for one in range(0, seqs, 2):
            products = lax.dot_general(
                key_ref[one * cache : (one + 2) * cache, both],
                spread,
                (((1,), (1,)), ((), ())),
                preferred_element_type=F32,
            )
            mine = jnp.where(lane_seq == one, products[:cache], products[cache:])
            scores = mine if one == 0 else jnp.where(lane_seq >= one, mine, scores)
        scores = scores * scale + bias_ref[...]
        peak = jnp.max(scores, axis=0, keepdims=True)
        raised = jnp.exp(scores - peak)
        probs = jnp.transpose(raised / jnp.sum(raised, axis=0, keepdims=True))
        apart = [jnp.where(row_seq == one, probs, 0.0).astype(BF16) for one in range(seqs)]
        out = jnp.dot(
            jnp.concatenate(apart, axis=1), value_ref[:, both], preferred_element_type=F32
        )
        out = out.astype(BF16).astype(F32)
        mixed += [
            out[k * each + h * seqs : k * each + (h + 1) * seqs, k * HD : (k + 1) * HD]
            for k in range(2)
            for h in range(group)
        ]
    start = pl.multiple_of(step * wide, wide)
    stream_ref[:, pl.ds(start, wide)] = residual + jnp.concatenate(mixed, axis=1)

    @pl.when(step == kvh // per_step - 1)
    def _():
        stream = stream_ref[...]
        width = stream.shape[1] // (pairs * reps)
        factor = lax.rsqrt(jnp.mean(stream * stream, axis=-1, keepdims=True) + 1e-05)
        for index, piece_ref in enumerate(piece_refs):
            dr, dp = divmod(index, pairs)
            column = lax.rem(lax.axis_index("pair") + dp, pairs) * reps
            column = column + lax.rem(lax.axis_index("rep") + dr, reps)
            own = pl.ds(pl.multiple_of(column * width, width), width)
            piece_ref[...] = (stream_ref[:, own] * factor * gain_ref[:, own]).astype(BF16)


def attend(cols, cache_len, query, key_cache, value_cache, residual, norm_gain):
    batches, _, rows, depth = query.shape
    seqs = batches * rows
    cache, kv = key_cache.shape[3:]
    kvh = kv // HD
    heads_per_step = 4
    wide = depth // kvh * heads_per_step
    columns = cols[0] * cols[1]
    by_head = pl.BlockSpec((batches, rows, wide), lambda i: (0, 0, i))
    cached = pl.BlockSpec((seqs * cache, heads_per_step * HD), lambda i: (0, i))
    return pl.pallas_call(
        functools.partial(attend_kernel, cols, kvh, heads_per_step),
        grid=(kvh // heads_per_step,),
        out_shape=[jax.ShapeDtypeStruct((seqs, depth), F32)]
        + [jax.ShapeDtypeStruct((seqs, depth // columns), BF16)] * columns,
        in_specs=[
            pl.BlockSpec(memory_space=SMEM),
            by_head,
            cached,
            cached,
            by_head,
            pl.BlockSpec((1, depth), lambda i: (0, 0)),
        ],
        out_specs=[pl.BlockSpec((seqs, depth), lambda i: (0, 0))]
        + [pl.BlockSpec((seqs, depth // columns), lambda i: (0, 0))] * columns,
        scratch_shapes=[pltpu.VMEM((cache, 2 * depth // kvh // HD * seqs), F32)],
        compiler_params=params(8),
        cost_estimate=cost(10**11),
        name="attend",
    )(
        cache_len.reshape(batches, rows),
        in_hbm(query.reshape(batches, rows, depth)),
        in_hbm(key_cache.reshape(seqs * cache, kv)),
        in_hbm(value_cache.reshape(seqs * cache, kv)),
        in_hbm(residual.reshape(batches, rows, depth)),
        in_hbm(norm_gain.reshape(1, depth)),
    )


def pack_kernel(cols, batches, table_ref, *refs):
    columns = cols[0] * cols[1]
    pieces = [ref[...].astype(F32) for ref in refs[:columns]]
    seqs = pieces[0].shape[0]
    row = lax.broadcasted_iota(jnp.int32, pieces[0].shape, 0)
    groups = [place_of(slot, cols, -1) for slot in range(columns)]
    picked = []
    for index in range(columns):
        column = place_of(index, cols)
        value = jnp.zeros_like(pieces[0])
        for micro in range(batches):
            taken = jnp.zeros_like(pieces[0])
            for slot in range(columns):
                taken = jnp.where(table_ref[micro, groups[slot]] == column, pieces[slot], taken)
            value = jnp.where(row >= micro * (seqs // batches), taken, value)
        picked.append(value)
    refs[columns][...] = jnp.concatenate(picked, axis=0).astype(BF16)


def pack(cols, batches, table, pieces):
    seqs, depth = pieces[0].shape
    return pl.pallas_call(
        functools.partial(pack_kernel, cols, batches),
        out_shape=jax.ShapeDtypeStruct((seqs * len(pieces), depth), BF16),
        in_specs=[TABLE] + [WHOLE] * len(pieces),
        out_specs=WHOLE,
        compiler_params=params(),
        cost_estimate=cost(),
        name="pack",
    )(table, *pieces)


def project_into(held, weight_ref, keep_ref, send_refs):
    half = keep_ref.shape[0]
    each = send_refs[0].shape[0]
    width = keep_ref.shape[1]
    tile = math.gcd(width, 256)
    for low in range(0, width, tile):
        part = slice(low, low + tile)
        sums = jnp.dot(held, weight_ref[:, part], preferred_element_type=F32)
        keep_ref[:, part] = sums[:half]
        for cut, send_ref in enumerate(send_refs):
            low_row = half + cut * each
            send_ref[:, part] = sums[low_row : low_row + each].astype(BF16)


def project_kernel(columns, count, cuts, weight_ref, *refs):
    keep_ref, *send_refs = refs[-1 - cuts :]
    packs = [ref[...].astype(F32) for ref in refs[:count]]
    rows = packs[0].shape[0] // columns
    held = [p[i * rows : (i + 1) * rows] for i in range(columns) for p in packs]
    held = jnp.concatenate(held, axis=0).astype(BF16)
    project_into(held, weight_ref, keep_ref, send_refs)


def sums_of(rows, width, reps, cuts):
    half = rows // reps
    return [
        jax.ShapeDtypeStruct((half, width), F32),
        *[jax.ShapeDtypeStruct(((rows - half) // cuts, width), BF16)] * cuts,
    ]


def project(cols, name, packs, weight, after, cuts=1, flops=LONG, kept=()):
    pairs, reps = cols
    rows = packs[0].shape[0] * len(packs)
    return pl.pallas_call(
        functools.partial(project_kernel, pairs * reps, len(packs), cuts),
        out_shape=sums_of(rows, weight.shape[1], reps, cuts),
        in_specs=[WHOLE] * (1 + len(packs)) + [UNREAD] * len(after) + [WHOLE] * len(kept),
        out_specs=[WHOLE] * (1 + cuts),
        compiler_params=params(),
        cost_estimate=cost(flops),
        name=name,
    )(weight, *packs, *after, *kept)


def mark_kernel(*refs):
    refs[-1][...] = jnp.zeros(refs[-1].shape, F32)


def mark(name, after, kept):
    return pl.pallas_call(
        mark_kernel,
        out_shape=jax.ShapeDtypeStruct((8, 128), F32),
        in_specs=[UNREAD] * len(after) + [WHOLE] * len(kept),
        out_specs=WHOLE,
        compiler_params=params(),
        cost_estimate=cost(LONG),
        name=name,
    )(*after, *kept)


def hold_kernel(*refs):
    refs[-1][...] = refs[0][...]


def hold(name, value, after):
    return pl.pallas_call(
        hold_kernel,
        out_shape=jax.ShapeDtypeStruct(value.shape, value.dtype),
        in_specs=[WHOLE] + [UNREAD] * len(after),
        out_specs=WHOLE,
        compiler_params=params(),
        cost_estimate=cost(LONG),
        name=name,
    )(value, *after)


def join_kernel(pairs, counts, *refs):
    outs = refs[-pairs:]
    rows = outs[0].shape[1]
    start = 0
    for place, count in enumerate(counts):
        keep_ref, *came_refs = refs[start : start + 1 + count]
        start += 1 + count
        came = jnp.concatenate([ref[...].astype(F32) for ref in came_refs], axis=0)
        outs[0][place] = keep_ref[:rows] + came[:rows]
        for dp in range(1, pairs):
            part = slice(dp * rows, (dp + 1) * rows)
            outs[dp][place] = (keep_ref[part] + came[part]).astype(BF16)


def join(pairs, name, sums, after):
    total, width = sums[0][0].shape
    shape = (2, total // pairs, width)
    counts = [len(item) - 1 for item in sums]
    flat = [part for item in sums for part in item]
    return pl.pallas_call(
        functools.partial(join_kernel, pairs, counts),
        out_shape=[jax.ShapeDtypeStruct(shape, F32)]
        + [jax.ShapeDtypeStruct(shape, BF16)] * (pairs - 1),
        in_specs=[WHOLE] * len(flat) + [UNREAD] * len(after),
        out_specs=[WHOLE] * pairs,
        compiler_params=params(),
        cost_estimate=cost(),
        name=name,
    )(*flat, *after)


def act_kernel(count, own_ref, *refs):
    sums = own_ref[...]
    for ref in refs[:count]:
        sums = sums + ref[...].astype(F32)
    gate = sums[0]
    refs[-1][...] = (gate / (1.0 + jnp.exp(-gate)) * sums[1]).astype(BF16)


def activate(name, own, arrived, after, flops=10**6):
    return pl.pallas_call(
        functools.partial(act_kernel, len(arrived)),
        out_shape=jax.ShapeDtypeStruct(own.shape[1:], BF16),
        in_specs=[WHOLE] * (1 + len(arrived)) + [UNREAD] * len(after),
        out_specs=WHOLE,
        compiler_params=params(),
        cost_estimate=cost(flops),
        name=name,
    )(own, *arrived, *after)


def served_kernel(batches, rows, *refs):
    out_ref = refs[-1]
    start = lax.axis_index("ffn") * rows
    parts = [ref[...].astype(F32) for ref in refs[:-1]]
    seqs = batches * rows
    for micro in range(batches):
        low = micro * rows
        mine = [p[s + low : s + low + rows] for p in parts for s in range(0, p.shape[0], seqs)]
        mine = jnp.concatenate(mine, axis=0)
        out_ref[micro, 0] = pltpu.roll(mine, start, 0).astype(BF16)


def serve(batches, rows, hidden):
    count, width = hidden[0].shape
    return pl.pallas_call(
        functools.partial(served_kernel, batches, rows),
        out_shape=jax.ShapeDtypeStruct((batches, 1, count * len(hidden) // batches, width), BF16),
        in_specs=[WHOLE] * len(hidden),
        out_specs=WHOLE,
        compiler_params=params(),
        cost_estimate=cost(),
        name="serve",
    )(*hidden)


def down_kernel(cols, batches, rows, sizes, skip, table_ref, weight_ref, *refs):
    pairs, reps = cols
    columns = pairs * reps
    count = columns * len(sizes)
    held = jnp.concatenate([ref[...] for ref in refs[:count]], axis=0)
    share_refs = refs[count + skip : -1]
    sums_ref = refs[-1]
    depth = weight_ref.shape[1]
    tile = math.gcd(depth, 256)
    for low in range(0, depth, tile):
        part = slice(low, low + tile)
        sums_ref[:, part] = jnp.dot(held, weight_ref[:, part], preferred_element_type=F32)
    seqs = batches * rows
    row = lax.broadcasted_iota(jnp.int32, (seqs, depth), 0)
    places = []
    for index in range(columns):
        held_at = []
        for micro in range(batches):
            column = table_ref[micro, place_of(index, cols)]
            to_pair = lax.rem(column // reps - lax.axis_index("pair") + pairs, pairs)
            to_rep = lax.rem(lax.rem(column, reps) - lax.axis_index("rep") + reps, reps)
            held_at.append(to_rep * pairs + to_pair)
        places.append(held_at)
    first = 0
    shift = 0
    for size in sizes:
        for inner in range(size // seqs):
            blocks = []
            for held_at in places:
                value = jnp.zeros((seqs, depth), F32)
                for micro, place in enumerate(held_at):
                    base = pl.multiple_of(first + place * size + inner * seqs, seqs)
                    value = jnp.where(row >= micro * rows, sums_ref[pl.ds(base, seqs), :], value)
                blocks.append(value)
            same = [blocks[dr * pairs] for dr in range(reps)]
            other = [blocks[dr * pairs + dp] for dp in range(1, pairs) for dr in range(reps)]
            share_refs[2 * shift][...] = jnp.concatenate(same, axis=0).astype(BF16)
            share_refs[2 * shift + 1][...] = jnp.concatenate(other, axis=0).astype(BF16)
            shift += 1
        first += columns * size


def down(cols, name, batches, rows, table, blocks, weight, after):
    pairs, reps = cols
    depth = weight.shape[1]
    seqs = batches * rows
    sizes = [block[0].shape[0] for block in blocks]
    shifts = sum(sizes) // seqs
    flat = [part for block in blocks for part in block]
    same = jax.ShapeDtypeStruct((reps * seqs, depth), BF16)
    other = jax.ShapeDtypeStruct(((pairs - 1) * reps * seqs, depth), BF16)
    out = pl.pallas_call(
        functools.partial(down_kernel, cols, batches, rows, sizes, len(after)),
        out_shape=[same, other] * shifts,
        in_specs=[TABLE] + [WHOLE] * (1 + len(flat)) + [UNREAD] * len(after),
        out_specs=[WHOLE] * (2 * shifts),
        scratch_shapes=[pltpu.VMEM((sum(sizes) * pairs * reps, depth), F32)],
        compiler_params=params(8),
        cost_estimate=cost(LONG),
        name=name,
    )(table, weight, *flat, *after)
    return out[0::2], out[1::2]


def total_kernel(count, outs, cuts, *refs):
    sums = refs[0][...].astype(F32)
    for ref in refs[1:count]:
        sums = sums + ref[...].astype(F32)
    rows, width = refs[-1].shape
    for index, out_ref in enumerate(refs[-outs:]):
        row, column = divmod(index, cuts)
        part = sums[row * rows : (row + 1) * rows, column * width : (column + 1) * width]
        out_ref[...] = part.astype(BF16)


def total(name, seqs, parts, after, cuts):
    rows, depth = parts[0].shape
    outs = rows // seqs * cuts
    return pl.pallas_call(
        functools.partial(total_kernel, len(parts), outs, cuts),
        out_shape=[jax.ShapeDtypeStruct((seqs, depth // cuts), BF16)] * outs,
        in_specs=[WHOLE] * len(parts) + [UNREAD] * len(after),
        out_specs=[WHOLE] * outs,
        compiler_params=params(),
        cost_estimate=cost(LONG),
        name=name,
    )(*parts, *after)


def finish_kernel(cols, pieces, stream_ref, *refs):
    out_ref = refs[-1]
    batches, _, rows, depth = out_ref.shape
    width = depth // (cols[0] * cols[1])
    start = 0
    for index, count in enumerate(pieces):
        column = place_of(index, cols, -1)
        for piece in range(count):
            ref = refs[start + piece]
            low = column * width + piece * (width // count)
            own = pl.ds(pl.multiple_of(low, width // count), width // count)
            sums = stream_ref[:, own] + ref[...].astype(F32)
            for micro in range(batches):
                out_ref[micro, 0, :, own] = sums[micro * rows : (micro + 1) * rows]
        start += count


def finish(cols, batches, stream, changes):
    seqs, depth = stream.shape
    flat = [part for parts in changes for part in parts]
    return pl.pallas_call(
        functools.partial(finish_kernel, cols, [len(parts) for parts in changes]),
        out_shape=jax.ShapeDtypeStruct((batches, 1, seqs // batches, depth), F32),
        in_specs=[WHOLE] * (1 + len(flat)),
        out_specs=WHOLE,
        compiler_params=params(),
        cost_estimate=cost(),
        name="finish",
    )(stream, *flat)


def to_column(cols, value, dr, dp):
    pairs, reps = cols
    route = [
        (p * reps + r, (p + dp) % pairs * reps + (r + dr) % reps)
        for p in range(pairs)
        for r in range(reps)
    ]
    return lax.ppermute(value, ("pair", "rep"), route)


def turn(value, ffn, shift):
    return lax.ppermute(value, "ffn", [(i, (i + shift) % ffn) for i in range(ffn)])


def per_device(
    cols,
    ffn,
    residual,
    query,
    key_cache,
    value_cache,
    cache_len,
    partner_table,
    norm_gain,
    gate_weight,
    up_weight,
    down_weight,
):
    pairs, reps = cols
    batches, _, rows, _ = query.shape
    stream, *normed = attend(
        cols, cache_len, query, key_cache, value_cache, residual, norm_gain
    )
    half = ffn // 2

    def spread(parts):
        return [to_column(cols, part, 0, dp + 1) for dp, part in enumerate(parts)]

    def swap(sums):
        return [sums[0], *[to_column(cols, part, 1, 0) for part in sums[1:]]]

    def collect(hidden):
        block = [hidden] + [to_column(cols, hidden, 0, pairs - dp) for dp in range(1, pairs)]
        return block + [to_column(cols, item, 1, 0) for item in block]

    mine = pack(cols, batches, partner_table, [
        to_column(cols, piece, *divmod(index, pairs)) if index else piece
        for index, piece in enumerate(normed)
    ])
    packs = [mine] + [turn(mine, ffn, -s) for s in range(1, ffn)]
    near, far = packs[:half], packs[half:]
    gate_near = project(cols, "gate_near", near, gate_weight, [], kept=[up_weight])
    up_near = project(cols, "up_near", near, up_weight, [])
    here = mark("far_here", far, [gate_weight, up_weight])
    near_own, *near_sent = join(pairs, "join_near", (swap(gate_near), swap(up_near)), [here])
    near_came = spread(near_sent)
    gate_far = project(cols, "gate_far", far, gate_weight, [near_own], pairs, kept=[up_weight])
    up_far = project(cols, "up_far", far, up_weight, [gate_far[0]], pairs, 10**6)
    near_hidden = activate("activate_near", near_own, near_came, [])
    far_own, *far_sent = join(
        pairs, "join_far", (swap(gate_far), swap(up_far)), [near_hidden]
    )
    far_came = spread(far_sent)
    far_hidden = activate("activate_far", far_own, far_came, [])
    hiddens = [near_hidden, far_hidden]
    blocks = [collect(hidden) for hidden in hiddens]
    shares = down(cols, "down", batches, rows, partner_table, blocks, down_weight, [])
    totals = []
    for kind in (1, 0):
        gathered = [shares[kind][0]] + [turn(shares[kind][s], ffn, s) for s in range(1, ffn)]
        after = [part for parts in totals for part in parts[:1]]
        name = ("total_same", "total_other")[kind]
        totals.append(total(name, batches * rows, gathered, after, 2 - kind))
    other, same = totals
    changes = []
    for dr in range(reps):
        parts = same[2 * dr : 2 * dr + 2]
        changes.append([to_column(cols, part, dr, 0) if dr else part for part in parts])
        for dp in range(1, pairs):
            changes.append([to_column(cols, other[(dp - 1) * reps + dr], dr, dp)])
    served = serve(batches, rows, hiddens)
    updated = finish(cols, batches, stream, changes)
    return (updated, served)


def solution(mesh):
    sizes = dict(mesh.shape)
    cols = (sizes["pair"], sizes["rep"])
    rows = P(None, ("parts", "pair", "rep"), "ffn", None)
    caches = P(None, ("parts", "pair", "rep"), "ffn", None, None)
    placed = (
        rows,
        rows,
        caches,
        caches,
        P(None, ("parts", "pair", "rep"), "ffn"),
        P("parts", None),
        P(),
        P(("pair", "rep"), "ffn"),
        P(("pair", "rep"), "ffn"),
        P("ffn", ("pair", "rep")),
    )
    return jax.shard_map(
        functools.partial(per_device, cols, sizes["ffn"]),
        mesh=mesh,
        in_specs=placed,
        out_specs=(rows, P(None, ("parts", "pair", "rep"), None, "ffn")),
        check_vma=False,
    )
```

```python
import functools
import math

import jax
import jax.numpy as jnp
from jax import lax
from jax.experimental import pallas as pl
from jax.experimental.pallas import tpu as pltpu
from jax.sharding import PartitionSpec as P

HD = 128
F32 = jnp.float32
BF16 = jnp.bfloat16
SMEM = pltpu.MemorySpace.SMEM
VMEM = pltpu.MemorySpace.VMEM
WHOLE = pl.BlockSpec(memory_space=VMEM)
UNREAD = pl.BlockSpec(memory_space=pl.ANY)
LONG = 5 * 10**10
TABLE = pl.BlockSpec(memory_space=SMEM)


def in_hbm(value):
    return pltpu.with_memory_space_constraint(value, pltpu.MemorySpace.HBM)


def params(size=4):
    return pltpu.CompilerParams(vmem_limit_bytes=size * 1024 * 1024)


def cost(flops=10**6):
    return pl.CostEstimate(flops=flops, bytes_accessed=flops // 1000, transcendentals=0)


def place_of(index, cols, sign=1):
    pairs, reps = cols
    dr, dp = divmod(index, pairs)
    pair = lax.rem(lax.axis_index("pair") + sign * dp + pairs, pairs)
    rep = lax.rem(lax.axis_index("rep") + sign * dr + reps, reps)
    return pair * reps + rep


def attend_kernel(
    cols, kvh, per_step, len_ref, query_ref, key_ref, value_ref, residual_ref, gain_ref, *refs
):
    pairs, reps = cols
    stream_ref = refs[0]
    piece_refs = refs[1 : 1 + pairs * reps]
    bias_ref, = refs[1 + pairs * reps :]
    step = pl.program_id(0)
    batches, rows, wide = query_ref.shape
    seqs = batches * rows
    cache = key_ref.shape[0] // seqs
    group = wide // (per_step * HD)
    each = group * seqs
    scale = 1.0 / math.sqrt(HD)

    @pl.when(step == 0)
    def _():
        seq = lax.rem(lax.broadcasted_iota(jnp.int32, bias_ref.shape, 1), seqs)
        place = lax.broadcasted_iota(jnp.int32, bias_ref.shape, 0)
        place = place.astype(F32)
        limit = jnp.zeros(bias_ref.shape, F32)
        for one in range(seqs):
            lengths = len_ref[one // rows].astype(F32)
            here = lax.broadcasted_iota(jnp.int32, lengths.shape, 1) == one % rows
            length = jnp.sum(jnp.where(here, lengths, 0.0), axis=1, keepdims=True)
            limit = jnp.where(seq == one, length, limit)
        bias_ref[...] = jnp.where(place < limit, 0.0, -1e30)

    queries = jnp.concatenate([query_ref[b].astype(F32) for b in range(batches)], axis=0)
    residual = jnp.concatenate([residual_ref[b] for b in range(batches)], axis=0)
    lane_seq = lax.rem(lax.broadcasted_iota(jnp.int32, (cache, 2 * each), 1), seqs)
    row_seq = lax.rem(lax.broadcasted_iota(jnp.int32, (2 * each, cache), 0), seqs)
    mixed = []
    for low in range(0, per_step, 2):
        both = slice(low * HD, (low + 2) * HD)
        blocks = []
        for k in range(2):
            heads = range((low + k) * group, (low + k + 1) * group)
            stacked = jnp.concatenate([queries[:, h * HD : (h + 1) * HD] for h in heads], axis=0)
            empty = jnp.zeros_like(stacked)
            blocks.append(jnp.concatenate([empty, stacked] if k else [stacked, empty], axis=1))
        spread = jnp.concatenate(blocks, axis=0).astype(BF16)
        scores = None
        for one in range(0, seqs, 2):
            products = lax.dot_general(
                key_ref[one * cache : (one + 2) * cache, both],
                spread,
                (((1,), (1,)), ((), ())),
                preferred_element_type=F32,
            )
            mine = jnp.where(lane_seq == one, products[:cache], products[cache:])
            scores = mine if one == 0 else jnp.where(lane_seq >= one, mine, scores)
        scores = scores * scale + bias_ref[...]
        peak = jnp.max(scores, axis=0, keepdims=True)
        raised = jnp.exp(scores - peak)
        probs = jnp.transpose(raised / jnp.sum(raised, axis=0, keepdims=True))
        apart = [jnp.where(row_seq == one, probs, 0.0).astype(BF16) for one in range(seqs)]
        out = jnp.dot(
            jnp.concatenate(apart, axis=1), value_ref[:, both], preferred_element_type=F32
        )
        out = out.astype(BF16).astype(F32)
        mixed += [
            out[k * each + h * seqs : k * each + (h + 1) * seqs, k * HD : (k + 1) * HD]
            for k in range(2)
            for h in range(group)
        ]
    start = pl.multiple_of(step * wide, wide)
    stream_ref[:, pl.ds(start, wide)] = residual + jnp.concatenate(mixed, axis=1)

    @pl.when(step == kvh // per_step - 1)
    def _():
        stream = stream_ref[...]
        width = stream.shape[1] // (pairs * reps)
        factor = lax.rsqrt(jnp.mean(stream * stream, axis=-1, keepdims=True) + 1e-05)
        for index, piece_ref in enumerate(piece_refs):
            dr, dp = divmod(index, pairs)
            column = lax.rem(lax.axis_index("pair") + dp, pairs) * reps
            column = column + lax.rem(lax.axis_index("rep") + dr, reps)
            own = pl.ds(pl.multiple_of(column * width, width), width)
            piece_ref[...] = (stream_ref[:, own] * factor * gain_ref[:, own]).astype(BF16)


def attend(cols, cache_len, query, key_cache, value_cache, residual, norm_gain):
    batches, _, rows, depth = query.shape
    seqs = batches * rows
    cache, kv = key_cache.shape[3:]
    kvh = kv // HD
    heads_per_step = 4
    wide = depth // kvh * heads_per_step
    columns = cols[0] * cols[1]
    by_head = pl.BlockSpec((batches, rows, wide), lambda i: (0, 0, i))
    cached = pl.BlockSpec((seqs * cache, heads_per_step * HD), lambda i: (0, i))
    return pl.pallas_call(
        functools.partial(attend_kernel, cols, kvh, heads_per_step),
        grid=(kvh // heads_per_step,),
        out_shape=[jax.ShapeDtypeStruct((seqs, depth), F32)]
        + [jax.ShapeDtypeStruct((seqs, depth // columns), BF16)] * columns,
        in_specs=[
            pl.BlockSpec(cache_len.shape, lambda i: (0, 0, 0)),
            by_head,
            cached,
            cached,
            by_head,
            pl.BlockSpec((1, depth), lambda i: (0, 0)),
        ],
        out_specs=[pl.BlockSpec((seqs, depth), lambda i: (0, 0))]
        + [pl.BlockSpec((seqs, depth // columns), lambda i: (0, 0))] * columns,
        scratch_shapes=[pltpu.VMEM((cache, 2 * depth // kvh // HD * seqs), F32)],
        compiler_params=params(8),
        cost_estimate=cost(10**11),
        name="attend",
    )(
        in_hbm(cache_len),
        in_hbm(query.reshape(batches, rows, depth)),
        in_hbm(key_cache.reshape(seqs * cache, kv)),
        in_hbm(value_cache.reshape(seqs * cache, kv)),
        in_hbm(residual.reshape(batches, rows, depth)),
        in_hbm(norm_gain.reshape(1, depth)),
    )


def pack_kernel(cols, batches, table_ref, *refs):
    columns = cols[0] * cols[1]
    pieces = [ref[...].astype(F32) for ref in refs[:columns]]
    seqs = pieces[0].shape[0]
    row = lax.broadcasted_iota(jnp.int32, pieces[0].shape, 0)
    groups = [place_of(slot, cols, -1) for slot in range(columns)]
    picked = []
    for index in range(columns):
        column = place_of(index, cols)
        value = None
        for micro in range(batches):
            taken = pieces[0]
            for slot in range(1, columns):
                taken = jnp.where(table_ref[micro, groups[slot]] == column, pieces[slot], taken)
            value = jnp.where(row >= micro * (seqs // batches), taken, value) if micro else taken
        picked.append(value)
    refs[columns][...] = jnp.concatenate(picked, axis=0).astype(BF16)


def pack(cols, batches, table, pieces):
    seqs, depth = pieces[0].shape
    return pl.pallas_call(
        functools.partial(pack_kernel, cols, batches),
        out_shape=jax.ShapeDtypeStruct((seqs * len(pieces), depth), BF16),
        in_specs=[TABLE] + [WHOLE] * len(pieces),
        out_specs=WHOLE,
        compiler_params=params(),
        cost_estimate=cost(),
        name="pack",
    )(table, *pieces)


def gate_up_kernel(columns, count, cuts, start, gate_ref, up_ref, *refs):
    keep_ref, *send_refs = refs[-1 - cuts :]
    if count > 1:
        packs = [ref[...].astype(F32) for ref in refs[:count]]
        rows = packs[0].shape[0] // columns
        held = [p[i * rows : (i + 1) * rows] for i in range(columns) for p in packs]
        refs[-2 - cuts][...] = jnp.concatenate(held, axis=0).astype(BF16)
        held = refs[-2 - cuts][...]
    else:
        held = refs[0][...]
    half, width = keep_ref.shape[1:]
    each = send_refs[0].shape[1]
    tile = math.gcd(width, 256)
    for place, weight_ref in enumerate((gate_ref, up_ref)):
        for low in range(0, width, tile):
            part = slice(low, low + tile)
            weight = weight_ref[:, start + low : start + low + tile]
            sums = jnp.dot(held, weight, preferred_element_type=F32)
            keep_ref[place, :, part] = sums[:half]
            for cut, send_ref in enumerate(send_refs):
                low_row = half + cut * each
                send_ref[place, :, part] = sums[low_row : low_row + each].astype(BF16)


def gate_up(cols, name, packs, weights, span, after, cuts, flops):
    pairs, reps = cols
    rows = packs[0].shape[0] * len(packs)
    half = rows // reps
    start, stop = span
    width = stop - start
    hand_on = [jax.ShapeDtypeStruct((rows, packs[0].shape[1]), BF16)] * (len(packs) > 1)
    return pl.pallas_call(
        functools.partial(gate_up_kernel, pairs * reps, len(packs), cuts, start),
        out_shape=hand_on
        + [
            jax.ShapeDtypeStruct((2, half, width), F32),
            *[jax.ShapeDtypeStruct((2, (rows - half) // cuts, width), BF16)] * cuts,
        ],
        in_specs=[WHOLE] * (2 + len(packs)) + [UNREAD] * len(after),
        out_specs=[WHOLE] * (len(hand_on) + 1 + cuts),
        compiler_params=params(),
        cost_estimate=cost(flops),
        name=name,
    )(*weights, *packs, *after)


def mark_kernel(*refs):
    refs[-1][...] = jnp.zeros(refs[-1].shape, F32)


def mark(name, after, kept):
    return pl.pallas_call(
        mark_kernel,
        out_shape=jax.ShapeDtypeStruct((8, 128), F32),
        in_specs=[UNREAD] * len(after) + [WHOLE] * len(kept),
        out_specs=WHOLE,
        compiler_params=params(),
        cost_estimate=cost(LONG),
        name=name,
    )(*after, *kept)


def hold_kernel(*refs):
    refs[-1][...] = refs[0][...]


def hold(name, value, after):
    return pl.pallas_call(
        hold_kernel,
        out_shape=jax.ShapeDtypeStruct(value.shape, value.dtype),
        in_specs=[WHOLE] + [UNREAD] * len(after),
        out_specs=WHOLE,
        compiler_params=params(),
        cost_estimate=cost(LONG),
        name=name,
    )(value, *after)


def join_kernel(pairs, counts, *refs):
    outs = refs[-pairs:]
    rows = outs[0].shape[1]
    start = 0
    low = 0
    for count in counts:
        keep_ref, *came_refs = refs[start : start + 1 + count]
        start += 1 + count
        came = jnp.concatenate([ref[...].astype(F32) for ref in came_refs], axis=1)
        part = slice(low, low + keep_ref.shape[2])
        low += keep_ref.shape[2]
        outs[0][:, :, part] = keep_ref[:, :rows] + came[:, :rows]
        for dp in range(1, pairs):
            block = slice(dp * rows, (dp + 1) * rows)
            outs[dp][:, :, part] = (keep_ref[:, block] + came[:, block]).astype(BF16)


def join(pairs, name, sums, after):
    width = sum(item[0].shape[2] for item in sums)
    shape = (2, sums[0][0].shape[1] // pairs, width)
    counts = [len(item) - 1 for item in sums]
    flat = [part for item in sums for part in item]
    return pl.pallas_call(
        functools.partial(join_kernel, pairs, counts),
        out_shape=[jax.ShapeDtypeStruct(shape, F32)]
        + [jax.ShapeDtypeStruct(shape, BF16)] * (pairs - 1),
        in_specs=[WHOLE] * len(flat) + [UNREAD] * len(after),
        out_specs=[WHOLE] * pairs,
        compiler_params=params(),
        cost_estimate=cost(),
        name=name,
    )(*flat, *after)


def act_kernel(count, own_ref, *refs):
    sums = own_ref[...]
    for ref in refs[:count]:
        sums = sums + ref[...].astype(F32)
    gate = sums[0]
    refs[-1][...] = (gate / (1.0 + jnp.exp(-gate)) * sums[1]).astype(BF16)


def activate(name, own, arrived, after, flops=10**6):
    return pl.pallas_call(
        functools.partial(act_kernel, len(arrived)),
        out_shape=jax.ShapeDtypeStruct(own.shape[1:], BF16),
        in_specs=[WHOLE] * (1 + len(arrived)) + [UNREAD] * len(after),
        out_specs=WHOLE,
        compiler_params=params(),
        cost_estimate=cost(flops),
        name=name,
    )(own, *arrived, *after)


def served_kernel(batches, rows, counts, *refs):
    out_ref = refs[-1]
    turned = lax.axis_index("ffn") * rows
    seqs = batches * rows
    groups = []
    start = 0
    for count in counts:
        parts = [ref[...].astype(F32) for ref in refs[start : start + count]]
        groups.append(jnp.concatenate(parts, axis=1))
        start += count
    for micro in range(batches):
        low = micro * rows
        mine = [p[s + low : s + low + rows] for p in groups for s in range(0, p.shape[0], seqs)]
        mine = jnp.concatenate(mine, axis=0)
        out_ref[micro, 0] = pltpu.roll(mine, turned, 0).astype(BF16)


def serve(batches, rows, hidden):
    flat = [part for group in hidden for part in group]
    width = sum(part.shape[1] for part in hidden[0])
    total_rows = sum(group[0].shape[0] for group in hidden)
    return pl.pallas_call(
        functools.partial(served_kernel, batches, rows, [len(group) for group in hidden]),
        out_shape=jax.ShapeDtypeStruct((batches, 1, total_rows // batches, width), BF16),
        in_specs=[WHOLE] * len(flat),
        out_specs=WHOLE,
        compiler_params=params(),
        cost_estimate=cost(),
        name="serve",
    )(*flat)


def down_kernel(cols, batches, rows, sizes, parts, skip, table_ref, weight_ref, *refs):
    pairs, reps = cols
    columns = pairs * reps
    count = columns * sum(parts)
    held = []
    start = 0
    for part_count in parts:
        wide = []
        for _ in range(part_count):
            wide.append(jnp.concatenate([ref[...] for ref in refs[start : start + columns]], axis=0))
            start += columns
        held.append(jnp.concatenate(wide, axis=1))
    held = jnp.concatenate(held, axis=0)
    share_refs = refs[count + skip : -1]
    sums_ref = refs[-1]
    depth = weight_ref.shape[1]
    tile = math.gcd(depth, 256)
    for low in range(0, depth, tile):
        part = slice(low, low + tile)
        sums_ref[:, part] = jnp.dot(held, weight_ref[:, part], preferred_element_type=F32)
    seqs = batches * rows
    row = lax.broadcasted_iota(jnp.int32, (seqs, depth), 0)
    places = []
    for index in range(columns):
        held_at = []
        for micro in range(batches):
            column = table_ref[micro, place_of(index, cols)]
            to_pair = lax.rem(column // reps - lax.axis_index("pair") + pairs, pairs)
            to_rep = lax.rem(lax.rem(column, reps) - lax.axis_index("rep") + reps, reps)
            held_at.append(to_rep * pairs + to_pair)
        places.append(held_at)
    first = 0
    shift = 0
    for size in sizes:
        for inner in range(size // seqs):
            blocks = []
            for held_at in places:
                value = None
                for micro, place in enumerate(held_at):
                    base = pl.multiple_of(first + place * size + inner * seqs, seqs)
                    found = sums_ref[pl.ds(base, seqs), :]
                    value = jnp.where(row >= micro * rows, found, value) if micro else found
                blocks.append(value)
            same = [blocks[dr * pairs] for dr in range(reps)]
            other = [blocks[dr * pairs + dp] for dp in range(1, pairs) for dr in range(reps)]
            share_refs[2 * shift][...] = jnp.concatenate(same, axis=0).astype(BF16)
            share_refs[2 * shift + 1][...] = jnp.concatenate(other, axis=0).astype(BF16)
            shift += 1
        first += columns * size


def down(cols, name, batches, rows, table, blocks, weight, after):
    pairs, reps = cols
    depth = weight.shape[1]
    seqs = batches * rows
    sizes = [group[0][0].shape[0] for group in blocks]
    parts = [len(group) for group in blocks]
    shifts = sum(sizes) // seqs
    flat = [item for group in blocks for block in group for item in block]
    same = jax.ShapeDtypeStruct((reps * seqs, depth), BF16)
    other = jax.ShapeDtypeStruct(((pairs - 1) * reps * seqs, depth), BF16)
    out = pl.pallas_call(
        functools.partial(down_kernel, cols, batches, rows, sizes, parts, len(after)),
        out_shape=[same, other] * shifts,
        in_specs=[TABLE] + [WHOLE] * (1 + len(flat)) + [UNREAD] * len(after),
        out_specs=[WHOLE] * (2 * shifts),
        scratch_shapes=[pltpu.VMEM((sum(sizes) * pairs * reps, depth), F32)],
        compiler_params=params(8),
        cost_estimate=cost(LONG),
        name=name,
    )(table, weight, *flat, *after)
    return out[0::2], out[1::2]


def total_kernel(count, outs, cuts, *refs):
    sums = refs[0][...].astype(F32)
    for ref in refs[1:count]:
        sums = sums + ref[...].astype(F32)
    rows, width = refs[-1].shape
    for index, out_ref in enumerate(refs[-outs:]):
        row, column = divmod(index, cuts)
        part = sums[row * rows : (row + 1) * rows, column * width : (column + 1) * width]
        out_ref[...] = part.astype(BF16)


def total(name, seqs, parts, after, cuts):
    rows, depth = parts[0].shape
    outs = rows // seqs * cuts
    return pl.pallas_call(
        functools.partial(total_kernel, len(parts), outs, cuts),
        out_shape=[jax.ShapeDtypeStruct((seqs, depth // cuts), BF16)] * outs,
        in_specs=[WHOLE] * len(parts) + [UNREAD] * len(after),
        out_specs=[WHOLE] * outs,
        compiler_params=params(),
        cost_estimate=cost(LONG),
        name=name,
    )(*parts, *after)


def finish_kernel(cols, pieces, stream_ref, *refs):
    out_ref = refs[-1]
    batches, _, rows, depth = out_ref.shape
    width = depth // (cols[0] * cols[1])
    start = 0
    for index, count in enumerate(pieces):
        column = place_of(index, cols, -1)
        for piece in range(count):
            ref = refs[start + piece]
            low = column * width + piece * (width // count)
            own = pl.ds(pl.multiple_of(low, width // count), width // count)
            sums = stream_ref[:, own] + ref[...].astype(F32)
            for micro in range(batches):
                out_ref[micro, 0, :, own] = sums[micro * rows : (micro + 1) * rows]
        start += count


def finish(cols, batches, stream, changes):
    seqs, depth = stream.shape
    flat = [part for parts in changes for part in parts]
    return pl.pallas_call(
        functools.partial(finish_kernel, cols, [len(parts) for parts in changes]),
        out_shape=jax.ShapeDtypeStruct((batches, 1, seqs // batches, depth), F32),
        in_specs=[WHOLE] * (1 + len(flat)),
        out_specs=WHOLE,
        compiler_params=params(),
        cost_estimate=cost(),
        name="finish",
    )(stream, *flat)


def to_column(cols, value, dr, dp):
    pairs, reps = cols
    route = [
        (p * reps + r, (p + dp) % pairs * reps + (r + dr) % reps)
        for p in range(pairs)
        for r in range(reps)
    ]
    return lax.ppermute(value, ("pair", "rep"), route)


def turn(value, ffn, shift):
    return lax.ppermute(value, "ffn", [(i, (i + shift) % ffn) for i in range(ffn)])


def per_device(
    cols,
    ffn,
    residual,
    query,
    key_cache,
    value_cache,
    cache_len,
    partner_table,
    norm_gain,
    gate_weight,
    up_weight,
    down_weight,
):
    pairs, reps = cols
    batches, _, rows, _ = query.shape
    stream, *normed = attend(
        cols, cache_len, query, key_cache, value_cache, residual, norm_gain
    )
    half = ffn // 2

    def spread(parts):
        return [to_column(cols, part, 0, dp + 1) for dp, part in enumerate(parts)]

    def swap(sums):
        return [sums[0], *[to_column(cols, part, 1, 0) for part in sums[1:]]]

    def collect(hidden):
        block = [hidden] + [to_column(cols, hidden, 0, pairs - dp) for dp in range(1, pairs)]
        return block + [to_column(cols, item, 1, 0) for item in block]

    mine = pack(cols, batches, partner_table, [
        to_column(cols, piece, *divmod(index, pairs)) if index else piece
        for index, piece in enumerate(normed)
    ])
    packs = [mine] + [turn(mine, ffn, -s) for s in range(1, ffn)]
    near, far = packs[:half], packs[half:]
    weights = (gate_weight, up_weight)
    units = gate_weight.shape[1] // 128
    edge = units // 2 * 128
    spans = ((0, edge), (edge, units * 128))
    held, *first = gate_up(cols, "gate_up_near_0", near, weights, spans[0], [], 1, LONG)
    second = gate_up(cols, "gate_up_near_1", [held], weights, spans[1], [], 1, LONG)
    here = mark("far_here", far, [])
    near_own, *near_sent = join(pairs, "join_near", [swap(first), swap(second)], [here])
    near_came = spread(near_sent)
    held, *first = gate_up(cols, "gate_up_far_0", far, weights, spans[0], [near_own], pairs, LONG)
    second = gate_up(cols, "gate_up_far_1", [held], weights, spans[1], [], pairs, 10**6)
    first_own, *first_sent = join(pairs, "join_far_0", [swap(first)], [])
    first_came = spread(first_sent)
    near_hidden = activate("activate_near", near_own, near_came, [first_own], LONG)
    second_own, *second_sent = join(pairs, "join_far_1", [swap(second)], [])
    second_came = spread(second_sent)
    first_hidden = activate("activate_far_0", first_own, first_came, [])
    second_hidden = activate("activate_far_1", second_own, second_came, [])
    hiddens = [[near_hidden], [first_hidden, second_hidden]]
    blocks = [[collect(part) for part in group] for group in hiddens]
    shares = down(cols, "down", batches, rows, partner_table, blocks, down_weight, [])
    totals = []
    for kind in (1, 0):
        gathered = [shares[kind][0]] + [turn(shares[kind][s], ffn, s) for s in range(1, ffn)]
        after = [part for parts in totals for part in parts[:1]]
        name = ("total_same", "total_other")[kind]
        totals.append(total(name, batches * rows, gathered, after, 2 - kind))
    other, same = totals
    changes = []
    for dr in range(reps):
        parts = same[2 * dr : 2 * dr + 2]
        changes.append([to_column(cols, part, dr, 0) if dr else part for part in parts])
        for dp in range(1, pairs):
            changes.append([to_column(cols, other[(dp - 1) * reps + dr], dr, dp)])
    served = serve(batches, rows, hiddens)
    updated = finish(cols, batches, stream, changes)
    return (updated, served)


def solution(mesh):
    sizes = dict(mesh.shape)
    cols = (sizes["pair"], sizes["rep"])
    rows = P(None, ("parts", "pair", "rep"), "ffn", None)
    caches = P(None, ("parts", "pair", "rep"), "ffn", None, None)
    placed = (
        rows,
        rows,
        caches,
        caches,
        P(None, ("parts", "pair", "rep"), "ffn"),
        P("parts", None),
        P(),
        P(("pair", "rep"), "ffn"),
        P(("pair", "rep"), "ffn"),
        P("ffn", ("pair", "rep")),
    )
    return jax.shard_map(
        functools.partial(per_device, cols, sizes["ffn"]),
        mesh=mesh,
        in_specs=placed,
        out_specs=(rows, P(None, ("parts", "pair", "rep"), None, "ffn")),
        check_vma=False,
    )
```

```python
import functools
import math

import jax
import jax.numpy as jnp
from jax import lax
from jax.experimental import pallas as pl
from jax.experimental.pallas import tpu as pltpu
from jax.sharding import PartitionSpec as P

HD = 128
F32 = jnp.float32
BF16 = jnp.bfloat16
SMEM = pltpu.MemorySpace.SMEM
VMEM = pltpu.MemorySpace.VMEM
WHOLE = pl.BlockSpec(memory_space=VMEM)
UNREAD = pl.BlockSpec(memory_space=pl.ANY)
LONG = 5 * 10**10
TABLE = pl.BlockSpec(memory_space=SMEM)


def in_hbm(value):
    return pltpu.with_memory_space_constraint(value, pltpu.MemorySpace.HBM)


def params(size=4):
    return pltpu.CompilerParams(vmem_limit_bytes=size * 1024 * 1024)


def cost(flops=10**6):
    return pl.CostEstimate(flops=flops, bytes_accessed=flops // 1000, transcendentals=0)


def place_of(index, cols, sign=1):
    pairs, reps = cols
    dr, dp = divmod(index, pairs)
    pair = lax.rem(lax.axis_index("pair") + sign * dp + pairs, pairs)
    rep = lax.rem(lax.axis_index("rep") + sign * dr + reps, reps)
    return pair * reps + rep


def attend_kernel(
    cols, kvh, per_step, len_ref, query_ref, key_ref, value_ref, residual_ref, gain_ref, *refs
):
    pairs, reps = cols
    stream_ref = refs[0]
    piece_refs = refs[1 : 1 + pairs * reps]
    bias_ref, = refs[1 + pairs * reps :]
    step = pl.program_id(0)
    batches, rows, wide = query_ref.shape
    seqs = batches * rows
    cache = key_ref.shape[0] // seqs
    group = wide // (per_step * HD)
    each = group * seqs
    scale = 1.0 / math.sqrt(HD)

    @pl.when(step == 0)
    def _():
        seq = lax.rem(lax.broadcasted_iota(jnp.int32, bias_ref.shape, 1), seqs)
        place = lax.broadcasted_iota(jnp.int32, bias_ref.shape, 0)
        place = place.astype(F32)
        limit = jnp.zeros(bias_ref.shape, F32)
        for one in range(seqs):
            lengths = len_ref[one // rows].astype(F32)
            here = lax.broadcasted_iota(jnp.int32, lengths.shape, 1) == one % rows
            length = jnp.sum(jnp.where(here, lengths, 0.0), axis=1, keepdims=True)
            limit = jnp.where(seq == one, length, limit)
        bias_ref[...] = jnp.where(place < limit, 0.0, -1e30)

    queries = jnp.concatenate([query_ref[b].astype(F32) for b in range(batches)], axis=0)
    residual = jnp.concatenate([residual_ref[b] for b in range(batches)], axis=0)
    lane_seq = lax.rem(lax.broadcasted_iota(jnp.int32, (cache, 2 * each), 1), seqs)
    row_seq = lax.rem(lax.broadcasted_iota(jnp.int32, (2 * each, cache), 0), seqs)
    mixed = []
    for low in range(0, per_step, 2):
        both = slice(low * HD, (low + 2) * HD)
        blocks = []
        for k in range(2):
            heads = range((low + k) * group, (low + k + 1) * group)
            stacked = jnp.concatenate([queries[:, h * HD : (h + 1) * HD] for h in heads], axis=0)
            empty = jnp.zeros_like(stacked)
            blocks.append(jnp.concatenate([empty, stacked] if k else [stacked, empty], axis=1))
        spread = jnp.concatenate(blocks, axis=0).astype(BF16)
        scores = None
        for one in range(0, seqs, 2):
            products = lax.dot_general(
                key_ref[one * cache : (one + 2) * cache, both],
                spread,
                (((1,), (1,)), ((), ())),
                preferred_element_type=F32,
            )
            mine = jnp.where(lane_seq == one, products[:cache], products[cache:])
            scores = mine if one == 0 else jnp.where(lane_seq >= one, mine, scores)
        scores = scores * scale + bias_ref[...]
        peak = jnp.max(scores, axis=0, keepdims=True)
        raised = jnp.exp(scores - peak)
        probs = jnp.transpose(raised / jnp.sum(raised, axis=0, keepdims=True))
        apart = [jnp.where(row_seq == one, probs, 0.0).astype(BF16) for one in range(seqs)]
        out = jnp.dot(
            jnp.concatenate(apart, axis=1), value_ref[:, both], preferred_element_type=F32
        )
        out = out.astype(BF16).astype(F32)
        mixed += [
            out[k * each + h * seqs : k * each + (h + 1) * seqs, k * HD : (k + 1) * HD]
            for k in range(2)
            for h in range(group)
        ]
    start = pl.multiple_of(step * wide, wide)
    stream_ref[:, pl.ds(start, wide)] = residual + jnp.concatenate(mixed, axis=1)

    @pl.when(step == kvh // per_step - 1)
    def _():
        stream = stream_ref[...]
        width = stream.shape[1] // (pairs * reps)
        factor = lax.rsqrt(jnp.mean(stream * stream, axis=-1, keepdims=True) + 1e-05)
        for index, piece_ref in enumerate(piece_refs):
            dr, dp = divmod(index, pairs)
            column = lax.rem(lax.axis_index("pair") + dp, pairs) * reps
            column = column + lax.rem(lax.axis_index("rep") + dr, reps)
            own = pl.ds(pl.multiple_of(column * width, width), width)
            piece_ref[...] = (stream_ref[:, own] * factor * gain_ref[:, own]).astype(BF16)


def attend(cols, cache_len, query, key_cache, value_cache, residual, norm_gain):
    batches, _, rows, depth = query.shape
    seqs = batches * rows
    cache, kv = key_cache.shape[3:]
    kvh = kv // HD
    heads_per_step = 4
    wide = depth // kvh * heads_per_step
    columns = cols[0] * cols[1]
    by_head = pl.BlockSpec((batches, rows, wide), lambda i: (0, 0, i))
    cached = pl.BlockSpec((seqs * cache, heads_per_step * HD), lambda i: (0, i))
    return pl.pallas_call(
        functools.partial(attend_kernel, cols, kvh, heads_per_step),
        grid=(kvh // heads_per_step,),
        out_shape=[jax.ShapeDtypeStruct((seqs, depth), F32)]
        + [jax.ShapeDtypeStruct((seqs, depth // columns), BF16)] * columns,
        in_specs=[
            pl.BlockSpec(cache_len.shape, lambda i: (0, 0, 0)),
            by_head,
            cached,
            cached,
            by_head,
            pl.BlockSpec((1, depth), lambda i: (0, 0)),
        ],
        out_specs=[pl.BlockSpec((seqs, depth), lambda i: (0, 0))]
        + [pl.BlockSpec((seqs, depth // columns), lambda i: (0, 0))] * columns,
        scratch_shapes=[pltpu.VMEM((cache, 2 * depth // kvh // HD * seqs), F32)],
        compiler_params=params(8),
        cost_estimate=cost(10**11),
        name="attend",
    )(
        in_hbm(cache_len),
        in_hbm(query.reshape(batches, rows, depth)),
        in_hbm(key_cache.reshape(seqs * cache, kv)),
        in_hbm(value_cache.reshape(seqs * cache, kv)),
        in_hbm(residual.reshape(batches, rows, depth)),
        in_hbm(norm_gain.reshape(1, depth)),
    )


def pack_kernel(cols, batches, table_ref, *refs):
    columns = cols[0] * cols[1]
    pieces = [ref[...].astype(F32) for ref in refs[:columns]]
    seqs = pieces[0].shape[0]
    row = lax.broadcasted_iota(jnp.int32, pieces[0].shape, 0)
    groups = [place_of(slot, cols, -1) for slot in range(columns)]
    picked = []
    for index in range(columns):
        column = place_of(index, cols)
        value = None
        for micro in range(batches):
            taken = pieces[0]
            for slot in range(1, columns):
                taken = jnp.where(table_ref[micro, groups[slot]] == column, pieces[slot], taken)
            value = jnp.where(row >= micro * (seqs // batches), taken, value) if micro else taken
        picked.append(value)
    refs[columns][...] = jnp.concatenate(picked, axis=0).astype(BF16)


def pack(cols, batches, table, pieces):
    seqs, depth = pieces[0].shape
    return pl.pallas_call(
        functools.partial(pack_kernel, cols, batches),
        out_shape=jax.ShapeDtypeStruct((seqs * len(pieces), depth), BF16),
        in_specs=[TABLE] + [WHOLE] * len(pieces),
        out_specs=WHOLE,
        compiler_params=params(),
        cost_estimate=cost(),
        name="pack",
    )(table, *pieces)


def gate_up_kernel(columns, count, cuts, start, gate_ref, up_ref, *refs):
    keep_ref, *send_refs = refs[-1 - cuts :]
    if count > 1:
        packs = [ref[...].astype(F32) for ref in refs[:count]]
        rows = packs[0].shape[0] // columns
        held = [p[i * rows : (i + 1) * rows] for i in range(columns) for p in packs]
        refs[-2 - cuts][...] = jnp.concatenate(held, axis=0).astype(BF16)
        held = refs[-2 - cuts][...]
    else:
        held = refs[0][...]
    half, width = keep_ref.shape[1:]
    each = send_refs[0].shape[1]
    tile = math.gcd(width, 256)
    for place, weight_ref in enumerate((gate_ref, up_ref)):
        for low in range(0, width, tile):
            part = slice(low, low + tile)
            weight = weight_ref[:, start + low : start + low + tile]
            sums = jnp.dot(held, weight, preferred_element_type=F32)
            keep_ref[place, :, part] = sums[:half]
            for cut, send_ref in enumerate(send_refs):
                low_row = half + cut * each
                send_ref[place, :, part] = sums[low_row : low_row + each].astype(BF16)


def gate_up(cols, name, packs, weights, span, after, cuts, flops):
    pairs, reps = cols
    rows = packs[0].shape[0] * len(packs)
    half = rows // reps
    start, stop = span
    width = stop - start
    hand_on = [jax.ShapeDtypeStruct((rows, packs[0].shape[1]), BF16)] * (len(packs) > 1)
    return pl.pallas_call(
        functools.partial(gate_up_kernel, pairs * reps, len(packs), cuts, start),
        out_shape=hand_on
        + [
            jax.ShapeDtypeStruct((2, half, width), F32),
            *[jax.ShapeDtypeStruct((2, (rows - half) // cuts, width), BF16)] * cuts,
        ],
        in_specs=[WHOLE] * (2 + len(packs)) + [UNREAD] * len(after),
        out_specs=[WHOLE] * (len(hand_on) + 1 + cuts),
        compiler_params=params(),
        cost_estimate=cost(flops),
        name=name,
    )(*weights, *packs, *after)


def mark_kernel(*refs):
    refs[-1][...] = jnp.zeros(refs[-1].shape, F32)


def mark(name, after, kept):
    return pl.pallas_call(
        mark_kernel,
        out_shape=jax.ShapeDtypeStruct((8, 128), F32),
        in_specs=[UNREAD] * len(after) + [WHOLE] * len(kept),
        out_specs=WHOLE,
        compiler_params=params(),
        cost_estimate=cost(LONG),
        name=name,
    )(*after, *kept)


def hold_kernel(*refs):
    refs[-1][...] = refs[0][...]


def hold(name, value, after):
    return pl.pallas_call(
        hold_kernel,
        out_shape=jax.ShapeDtypeStruct(value.shape, value.dtype),
        in_specs=[WHOLE] + [UNREAD] * len(after),
        out_specs=WHOLE,
        compiler_params=params(),
        cost_estimate=cost(LONG),
        name=name,
    )(value, *after)


def join_kernel(pairs, counts, *refs):
    outs = refs[-pairs:]
    rows = outs[0].shape[1]
    start = 0
    low = 0
    for count in counts:
        keep_ref, *came_refs = refs[start : start + 1 + count]
        start += 1 + count
        came = jnp.concatenate([ref[...].astype(F32) for ref in came_refs], axis=1)
        part = slice(low, low + keep_ref.shape[2])
        low += keep_ref.shape[2]
        outs[0][:, :, part] = keep_ref[:, :rows] + came[:, :rows]
        for dp in range(1, pairs):
            block = slice(dp * rows, (dp + 1) * rows)
            outs[dp][:, :, part] = (keep_ref[:, block] + came[:, block]).astype(BF16)


def join(pairs, name, sums, after):
    width = sum(item[0].shape[2] for item in sums)
    shape = (2, sums[0][0].shape[1] // pairs, width)
    counts = [len(item) - 1 for item in sums]
    flat = [part for item in sums for part in item]
    return pl.pallas_call(
        functools.partial(join_kernel, pairs, counts),
        out_shape=[jax.ShapeDtypeStruct(shape, F32)]
        + [jax.ShapeDtypeStruct(shape, BF16)] * (pairs - 1),
        in_specs=[WHOLE] * len(flat) + [UNREAD] * len(after),
        out_specs=[WHOLE] * pairs,
        compiler_params=params(),
        cost_estimate=cost(),
        name=name,
    )(*flat, *after)


def act_kernel(count, own_ref, *refs):
    sums = own_ref[...]
    for ref in refs[:count]:
        sums = sums + ref[...].astype(F32)
    gate = sums[0]
    refs[-1][...] = (gate / (1.0 + jnp.exp(-gate)) * sums[1]).astype(BF16)


def activate(name, own, arrived, after, flops=10**6):
    return pl.pallas_call(
        functools.partial(act_kernel, len(arrived)),
        out_shape=jax.ShapeDtypeStruct(own.shape[1:], BF16),
        in_specs=[WHOLE] * (1 + len(arrived)) + [UNREAD] * len(after),
        out_specs=WHOLE,
        compiler_params=params(),
        cost_estimate=cost(flops),
        name=name,
    )(own, *arrived, *after)


def served_kernel(batches, rows, counts, *refs):
    out_ref, mark_ref = refs[-2:]
    mark_ref[...] = jnp.zeros(mark_ref.shape, F32)
    turned = lax.axis_index("ffn") * rows
    seqs = batches * rows
    groups = []
    start = 0
    for count in counts:
        parts = [ref[...].astype(F32) for ref in refs[start : start + count]]
        groups.append(jnp.concatenate(parts, axis=1))
        start += count
    for micro in range(batches):
        low = micro * rows
        mine = [p[s + low : s + low + rows] for p in groups for s in range(0, p.shape[0], seqs)]
        mine = jnp.concatenate(mine, axis=0)
        out_ref[micro, 0] = pltpu.roll(mine, turned, 0).astype(BF16)


def serve(batches, rows, hidden):
    flat = [part for group in hidden for part in group]
    width = sum(part.shape[1] for part in hidden[0])
    total_rows = sum(group[0].shape[0] for group in hidden)
    return pl.pallas_call(
        functools.partial(served_kernel, batches, rows, [len(group) for group in hidden]),
        out_shape=[
            jax.ShapeDtypeStruct((batches, 1, total_rows // batches, width), BF16),
            jax.ShapeDtypeStruct((8, 128), F32),
        ],
        in_specs=[WHOLE] * len(flat),
        out_specs=[WHOLE] * 2,
        compiler_params=params(),
        cost_estimate=cost(LONG),
        name="serve",
    )(*flat)


def down_kernel(cols, batches, rows, sizes, parts, skip, table_ref, weight_ref, *refs):
    pairs, reps = cols
    columns = pairs * reps
    count = columns * sum(parts)
    held = []
    start = 0
    for part_count in parts:
        wide = []
        for _ in range(part_count):
            wide.append(jnp.concatenate([ref[...] for ref in refs[start : start + columns]], axis=0))
            start += columns
        held.append(jnp.concatenate(wide, axis=1))
    held = jnp.concatenate(held, axis=0)
    share_refs = refs[count + skip : -1]
    sums_ref = refs[-1]
    depth = weight_ref.shape[1]
    tile = math.gcd(depth, 256)
    for low in range(0, depth, tile):
        part = slice(low, low + tile)
        sums_ref[:, part] = jnp.dot(held, weight_ref[:, part], preferred_element_type=F32)
    seqs = batches * rows
    row = lax.broadcasted_iota(jnp.int32, (seqs, depth), 0)
    places = []
    for index in range(columns):
        held_at = []
        for micro in range(batches):
            column = table_ref[micro, place_of(index, cols)]
            to_pair = lax.rem(column // reps - lax.axis_index("pair") + pairs, pairs)
            to_rep = lax.rem(lax.rem(column, reps) - lax.axis_index("rep") + reps, reps)
            held_at.append(to_rep * pairs + to_pair)
        places.append(held_at)
    count = sum(sizes) // seqs
    mine_refs, peer_refs = share_refs[:count], share_refs[count : count + reps - 1]
    other_refs = share_refs[count + reps - 1 :]
    first = 0
    shift = 0
    for size in sizes:
        for inner in range(size // seqs):
            blocks = []
            for held_at in places:
                value = None
                for micro, place in enumerate(held_at):
                    base = pl.multiple_of(first + place * size + inner * seqs, seqs)
                    found = sums_ref[pl.ds(base, seqs), :]
                    value = jnp.where(row >= micro * rows, found, value) if micro else found
                blocks.append(value)
            mine_refs[shift][...] = blocks[0].astype(BF16)
            for dr in range(1, reps):
                peer_refs[dr - 1][shift] = blocks[dr * pairs].astype(BF16)
            other = [blocks[dr * pairs + dp] for dp in range(1, pairs) for dr in range(reps)]
            other_refs[shift][...] = jnp.concatenate(other, axis=0).astype(BF16)
            shift += 1
        first += columns * size


def down(cols, name, batches, rows, table, blocks, weight, after):
    pairs, reps = cols
    depth = weight.shape[1]
    seqs = batches * rows
    sizes = [group[0][0].shape[0] for group in blocks]
    parts = [len(group) for group in blocks]
    shifts = sum(sizes) // seqs
    flat = [item for group in blocks for block in group for item in block]
    mine = jax.ShapeDtypeStruct((seqs, depth), BF16)
    peer = jax.ShapeDtypeStruct((shifts, seqs, depth), BF16)
    other = jax.ShapeDtypeStruct(((pairs - 1) * reps * seqs, depth), BF16)
    out = pl.pallas_call(
        functools.partial(down_kernel, cols, batches, rows, sizes, parts, len(after)),
        out_shape=[mine] * shifts + [peer] * (reps - 1) + [other] * shifts,
        in_specs=[TABLE] + [WHOLE] * (1 + len(flat)) + [UNREAD] * len(after),
        out_specs=[WHOLE] * (2 * shifts + reps - 1),
        scratch_shapes=[pltpu.VMEM((sum(sizes) * pairs * reps, depth), F32)],
        compiler_params=params(8),
        cost_estimate=cost(LONG),
        name=name,
    )(table, weight, *flat, *after)
    return out[:shifts], out[shifts : shifts + reps - 1], out[shifts + reps - 1 :]


def merge_kernel(shifts, reps, *refs):
    out_refs = refs[-shifts:]
    for shift, out_ref in enumerate(out_refs):
        out_ref[0] = refs[shift][...]
        for dr in range(1, reps):
            out_ref[dr] = refs[shifts + dr - 1][shift]


def merge(mine, peers, after):
    shifts, reps = len(mine), len(peers) + 1
    return pl.pallas_call(
        functools.partial(merge_kernel, shifts, reps),
        out_shape=[jax.ShapeDtypeStruct((reps, *mine[0].shape), BF16)] * shifts,
        in_specs=[WHOLE] * (shifts + reps - 1) + [UNREAD] * len(after),
        out_specs=[WHOLE] * shifts,
        compiler_params=params(),
        cost_estimate=cost(),
        name="merge",
    )(*mine, *peers, *after)


def total_kernel(count, outs, *refs):
    sums = refs[0][...].astype(F32)
    for ref in refs[1:count]:
        sums = sums + ref[...].astype(F32)
    if sums.ndim == 2:
        sums = sums.reshape(outs, sums.shape[0] // outs, sums.shape[1])
    for index, out_ref in enumerate(refs[-outs:]):
        out_ref[...] = sums[index].astype(BF16)


def total(name, seqs, parts, after):
    outs = parts[0].size // parts[0].shape[-1] // seqs
    return pl.pallas_call(
        functools.partial(total_kernel, len(parts), outs),
        out_shape=[jax.ShapeDtypeStruct((seqs, parts[0].shape[-1]), BF16)] * outs,
        in_specs=[WHOLE] * len(parts) + [UNREAD] * len(after),
        out_specs=[WHOLE] * outs,
        compiler_params=params(),
        cost_estimate=cost(LONG),
        name=name,
    )(*parts, *after)


def finish_kernel(cols, pieces, stream_ref, *refs):
    out_ref = refs[-1]
    batches, _, rows, depth = out_ref.shape
    width = depth // (cols[0] * cols[1])
    start = 0
    for index, count in enumerate(pieces):
        column = place_of(index, cols, -1)
        for piece in range(count):
            ref = refs[start + piece]
            low = column * width + piece * (width // count)
            own = pl.ds(pl.multiple_of(low, width // count), width // count)
            sums = stream_ref[:, own] + ref[...].astype(F32)
            for micro in range(batches):
                out_ref[micro, 0, :, own] = sums[micro * rows : (micro + 1) * rows]
        start += count


def finish(cols, batches, stream, changes):
    seqs, depth = stream.shape
    flat = [part for parts in changes for part in parts]
    return pl.pallas_call(
        functools.partial(finish_kernel, cols, [len(parts) for parts in changes]),
        out_shape=jax.ShapeDtypeStruct((batches, 1, seqs // batches, depth), F32),
        in_specs=[WHOLE] * (1 + len(flat)),
        out_specs=WHOLE,
        compiler_params=params(),
        cost_estimate=cost(),
        name="finish",
    )(stream, *flat)


def to_column(cols, value, dr, dp):
    pairs, reps = cols
    route = [
        (p * reps + r, (p + dp) % pairs * reps + (r + dr) % reps)
        for p in range(pairs)
        for r in range(reps)
    ]
    return lax.ppermute(value, ("pair", "rep"), route)


def turn(value, ffn, shift):
    return lax.ppermute(value, "ffn", [(i, (i + shift) % ffn) for i in range(ffn)])


def per_device(
    cols,
    ffn,
    residual,
    query,
    key_cache,
    value_cache,
    cache_len,
    partner_table,
    norm_gain,
    gate_weight,
    up_weight,
    down_weight,
):
    pairs, reps = cols
    batches, _, rows, _ = query.shape
    stream, *normed = attend(
        cols, cache_len, query, key_cache, value_cache, residual, norm_gain
    )
    half = ffn // 2

    def spread(parts):
        return [to_column(cols, part, 0, dp + 1) for dp, part in enumerate(parts)]

    def swap(sums):
        return [sums[0], *[to_column(cols, part, 1, 0) for part in sums[1:]]]

    def collect(hidden):
        block = [hidden] + [to_column(cols, hidden, 0, pairs - dp) for dp in range(1, pairs)]
        return block + [to_column(cols, item, 1, 0) for item in block]

    mine = pack(cols, batches, partner_table, [
        to_column(cols, piece, *divmod(index, pairs)) if index else piece
        for index, piece in enumerate(normed)
    ])
    packs = [mine] + [turn(mine, ffn, -s) for s in range(1, ffn)]
    near, far = packs[:half], packs[half:]
    weights = (gate_weight, up_weight)
    units = gate_weight.shape[1] // 128
    edge = units // 2 * 128
    spans = ((0, edge), (edge, units * 128))
    held, *first = gate_up(cols, "gate_up_near_0", near, weights, spans[0], [], 1, LONG)
    second = gate_up(cols, "gate_up_near_1", [held], weights, spans[1], [], 1, LONG)
    here = mark("far_here", far, [])
    near_own, *near_sent = join(pairs, "join_near", [swap(first), swap(second)], [here])
    near_came = spread(near_sent)
    held, *first = gate_up(cols, "gate_up_far_0", far, weights, spans[0], [near_own], pairs, LONG)
    second = gate_up(cols, "gate_up_far_1", [held], weights, spans[1], [], pairs, 10**6)
    first_own, *first_sent = join(pairs, "join_far_0", [swap(first)], [])
    first_came = spread(first_sent)
    near_hidden = activate("activate_near", near_own, near_came, [first_own], LONG)
    second_own, *second_sent = join(pairs, "join_far_1", [swap(second)], [])
    second_came = spread(second_sent)
    first_hidden = activate("activate_far_0", first_own, first_came, [])
    second_hidden = activate("activate_far_1", second_own, second_came, [])
    hiddens = [[near_hidden], [first_hidden, second_hidden]]
    blocks = [[collect(part) for part in group] for group in hiddens]
    served, placed = serve(batches, rows, hiddens)
    mine, peers, other = down(cols, "down", batches, rows, partner_table, blocks, down_weight, [])
    other = [other[0]] + [turn(other[s], ffn, s) for s in range(1, ffn)]
    same = merge(
        mine, [to_column(cols, peer, dr + 1, 0) for dr, peer in enumerate(peers)], [placed]
    )
    same = [same[0]] + [turn(same[s], ffn, s) for s in range(1, ffn)]
    other = total("total_other", batches * rows, other, [same[0]])
    same = total("total_same", batches * rows, same, other[:1])
    changes = []
    for dr in range(reps):
        changes.append([same[dr]])
        for dp in range(1, pairs):
            changes.append([to_column(cols, other[(dp - 1) * reps + dr], dr, dp)])
    updated = finish(cols, batches, stream, changes)
    return (updated, served)


def solution(mesh):
    sizes = dict(mesh.shape)
    cols = (sizes["pair"], sizes["rep"])
    rows = P(None, ("parts", "pair", "rep"), "ffn", None)
    caches = P(None, ("parts", "pair", "rep"), "ffn", None, None)
    placed = (
        rows,
        rows,
        caches,
        caches,
        P(None, ("parts", "pair", "rep"), "ffn"),
        P("parts", None),
        P(),
        P(("pair", "rep"), "ffn"),
        P(("pair", "rep"), "ffn"),
        P("ffn", ("pair", "rep")),
    )
    return jax.shard_map(
        functools.partial(per_device, cols, sizes["ffn"]),
        mesh=mesh,
        in_specs=placed,
        out_specs=(rows, P(None, ("parts", "pair", "rep"), None, "ffn")),
        check_vma=False,
    )
```

```python
import functools
import math

import jax
import jax.numpy as jnp
from jax import lax
from jax.experimental import pallas as pl
from jax.experimental.pallas import tpu as pltpu
from jax.sharding import PartitionSpec as P

HD = 128
F32 = jnp.float32
BF16 = jnp.bfloat16
SMEM = pltpu.MemorySpace.SMEM
VMEM = pltpu.MemorySpace.VMEM
WHOLE = pl.BlockSpec(memory_space=VMEM)
UNREAD = pl.BlockSpec(memory_space=pl.ANY)
LONG = 5 * 10**10
TABLE = pl.BlockSpec(memory_space=SMEM)


def in_hbm(value):
    return pltpu.with_memory_space_constraint(value, pltpu.MemorySpace.HBM)


def params(size=4):
    return pltpu.CompilerParams(vmem_limit_bytes=size * 1024 * 1024)


def cost(flops=10**6):
    return pl.CostEstimate(flops=flops, bytes_accessed=flops // 1000, transcendentals=0)


def place_of(index, cols, sign=1):
    pairs, reps = cols
    dr, dp = divmod(index, pairs)
    pair = lax.rem(lax.axis_index("pair") + sign * dp + pairs, pairs)
    rep = lax.rem(lax.axis_index("rep") + sign * dr + reps, reps)
    return pair * reps + rep


def attend_kernel(
    cols, kvh, per_step, len_ref, query_ref, key_ref, value_ref, residual_ref, gain_ref, *refs
):
    pairs, reps = cols
    stream_ref = refs[0]
    piece_refs = refs[1 : 1 + pairs * reps]
    bias_ref, = refs[1 + pairs * reps :]
    step = pl.program_id(0)
    batches, rows, wide = query_ref.shape
    seqs = batches * rows
    cache = key_ref.shape[0] // seqs
    group = wide // (per_step * HD)
    each = group * seqs
    scale = 1.0 / math.sqrt(HD)

    @pl.when(step == 0)
    def _():
        seq = lax.rem(lax.broadcasted_iota(jnp.int32, bias_ref.shape, 1), seqs)
        place = lax.broadcasted_iota(jnp.int32, bias_ref.shape, 0)
        place = place.astype(F32)
        limit = jnp.zeros(bias_ref.shape, F32)
        for one in range(seqs):
            lengths = len_ref[one // rows].astype(F32)
            here = lax.broadcasted_iota(jnp.int32, lengths.shape, 1) == one % rows
            length = jnp.sum(jnp.where(here, lengths, 0.0), axis=1, keepdims=True)
            limit = jnp.where(seq == one, length, limit)
        bias_ref[...] = jnp.where(place < limit, 0.0, -1e30)

    queries = jnp.concatenate([query_ref[b].astype(F32) for b in range(batches)], axis=0)
    residual = jnp.concatenate([residual_ref[b] for b in range(batches)], axis=0)
    lane_seq = lax.rem(lax.broadcasted_iota(jnp.int32, (cache, 2 * each), 1), seqs)
    row_seq = lax.rem(lax.broadcasted_iota(jnp.int32, (2 * each, cache), 0), seqs)
    mixed = []
    for low in range(0, per_step, 2):
        both = slice(low * HD, (low + 2) * HD)
        blocks = []
        for k in range(2):
            heads = range((low + k) * group, (low + k + 1) * group)
            stacked = jnp.concatenate([queries[:, h * HD : (h + 1) * HD] for h in heads], axis=0)
            empty = jnp.zeros_like(stacked)
            blocks.append(jnp.concatenate([empty, stacked] if k else [stacked, empty], axis=1))
        spread = jnp.concatenate(blocks, axis=0).astype(BF16)
        scores = None
        for one in range(0, seqs, 2):
            products = lax.dot_general(
                key_ref[one * cache : (one + 2) * cache, both],
                spread,
                (((1,), (1,)), ((), ())),
                preferred_element_type=F32,
            )
            mine = jnp.where(lane_seq == one, products[:cache], products[cache:])
            scores = mine if one == 0 else jnp.where(lane_seq >= one, mine, scores)
        scores = scores * scale + bias_ref[...]
        peak = jnp.max(scores, axis=0, keepdims=True)
        raised = jnp.exp(scores - peak)
        probs = jnp.transpose(raised / jnp.sum(raised, axis=0, keepdims=True))
        apart = [jnp.where(row_seq == one, probs, 0.0).astype(BF16) for one in range(seqs)]
        out = jnp.dot(
            jnp.concatenate(apart, axis=1), value_ref[:, both], preferred_element_type=F32
        )
        out = out.astype(BF16).astype(F32)
        mixed += [
            out[k * each + h * seqs : k * each + (h + 1) * seqs, k * HD : (k + 1) * HD]
            for k in range(2)
            for h in range(group)
        ]
    start = pl.multiple_of(step * wide, wide)
    stream_ref[:, pl.ds(start, wide)] = residual + jnp.concatenate(mixed, axis=1)

    @pl.when(step == kvh // per_step - 1)
    def _():
        stream = stream_ref[...]
        width = stream.shape[1] // (pairs * reps)
        factor = lax.rsqrt(jnp.mean(stream * stream, axis=-1, keepdims=True) + 1e-05)
        for index, piece_ref in enumerate(piece_refs):
            dr, dp = divmod(index, pairs)
            column = lax.rem(lax.axis_index("pair") + dp, pairs) * reps
            column = column + lax.rem(lax.axis_index("rep") + dr, reps)
            own = pl.ds(pl.multiple_of(column * width, width), width)
            piece_ref[...] = (stream_ref[:, own] * factor * gain_ref[:, own]).astype(BF16)


def attend(cols, cache_len, query, key_cache, value_cache, residual, norm_gain):
    batches, _, rows, depth = query.shape
    seqs = batches * rows
    cache, kv = key_cache.shape[3:]
    kvh = kv // HD
    heads_per_step = 4
    wide = depth // kvh * heads_per_step
    columns = cols[0] * cols[1]
    by_head = pl.BlockSpec((batches, rows, wide), lambda i: (0, 0, i))
    cached = pl.BlockSpec((seqs * cache, heads_per_step * HD), lambda i: (0, i))
    return pl.pallas_call(
        functools.partial(attend_kernel, cols, kvh, heads_per_step),
        grid=(kvh // heads_per_step,),
        out_shape=[jax.ShapeDtypeStruct((seqs, depth), F32)]
        + [jax.ShapeDtypeStruct((seqs, depth // columns), BF16)] * columns,
        in_specs=[
            pl.BlockSpec(cache_len.shape, lambda i: (0, 0, 0)),
            by_head,
            cached,
            cached,
            by_head,
            pl.BlockSpec((1, depth), lambda i: (0, 0)),
        ],
        out_specs=[pl.BlockSpec((seqs, depth), lambda i: (0, 0))]
        + [pl.BlockSpec((seqs, depth // columns), lambda i: (0, 0))] * columns,
        scratch_shapes=[pltpu.VMEM((cache, 2 * depth // kvh // HD * seqs), F32)],
        compiler_params=params(8),
        cost_estimate=cost(10**11),
        name="attend",
    )(
        in_hbm(cache_len),
        in_hbm(query.reshape(batches, rows, depth)),
        in_hbm(key_cache.reshape(seqs * cache, kv)),
        in_hbm(value_cache.reshape(seqs * cache, kv)),
        in_hbm(residual.reshape(batches, rows, depth)),
        in_hbm(norm_gain.reshape(1, depth)),
    )


def pack_kernel(cols, batches, table_ref, *refs):
    columns = cols[0] * cols[1]
    pieces = [ref[...].astype(F32) for ref in refs[:columns]]
    seqs = pieces[0].shape[0]
    row = lax.broadcasted_iota(jnp.int32, pieces[0].shape, 0)
    groups = [place_of(slot, cols, -1) for slot in range(columns)]
    picked = []
    for index in range(columns):
        column = place_of(index, cols)
        value = None
        for micro in range(batches):
            taken = pieces[0]
            for slot in range(1, columns):
                taken = jnp.where(table_ref[micro, groups[slot]] == column, pieces[slot], taken)
            value = jnp.where(row >= micro * (seqs // batches), taken, value) if micro else taken
        picked.append(value)
    refs[columns][...] = jnp.concatenate(picked, axis=0).astype(BF16)


def pack(cols, batches, table, pieces):
    seqs, depth = pieces[0].shape
    return pl.pallas_call(
        functools.partial(pack_kernel, cols, batches),
        out_shape=jax.ShapeDtypeStruct((seqs * len(pieces), depth), BF16),
        in_specs=[TABLE] + [WHOLE] * len(pieces),
        out_specs=WHOLE,
        compiler_params=params(),
        cost_estimate=cost(),
        name="pack",
    )(table, *pieces)


def gate_up_kernel(columns, count, cuts, start, gate_ref, up_ref, *refs):
    keep_ref, *send_refs = refs[-1 - cuts :]
    if count > 1:
        packs = [ref[...].astype(F32) for ref in refs[:count]]
        rows = packs[0].shape[0] // columns
        held = [p[i * rows : (i + 1) * rows] for i in range(columns) for p in packs]
        refs[-2 - cuts][...] = jnp.concatenate(held, axis=0).astype(BF16)
        held = refs[-2 - cuts][...]
    else:
        held = refs[0][...]
    half, width = keep_ref.shape[1:]
    each = send_refs[0].shape[1]
    tile = math.gcd(width, 256)
    for place, weight_ref in enumerate((gate_ref, up_ref)):
        for low in range(0, width, tile):
            part = slice(low, low + tile)
            weight = weight_ref[:, start + low : start + low + tile]
            sums = jnp.dot(held, weight, preferred_element_type=F32)
            keep_ref[place, :, part] = sums[:half]
            for cut, send_ref in enumerate(send_refs):
                low_row = half + cut * each
                send_ref[place, :, part] = sums[low_row : low_row + each].astype(BF16)


def gate_up(cols, name, packs, weights, span, after, cuts, flops):
    pairs, reps = cols
    rows = packs[0].shape[0] * len(packs)
    half = rows // reps
    start, stop = span
    width = stop - start
    hand_on = [jax.ShapeDtypeStruct((rows, packs[0].shape[1]), BF16)] * (len(packs) > 1)
    return pl.pallas_call(
        functools.partial(gate_up_kernel, pairs * reps, len(packs), cuts, start),
        out_shape=hand_on
        + [
            jax.ShapeDtypeStruct((2, half, width), F32),
            *[jax.ShapeDtypeStruct((2, (rows - half) // cuts, width), BF16)] * cuts,
        ],
        in_specs=[WHOLE] * (2 + len(packs)) + [UNREAD] * len(after),
        out_specs=[WHOLE] * (len(hand_on) + 1 + cuts),
        compiler_params=params(),
        cost_estimate=cost(flops),
        name=name,
    )(*weights, *packs, *after)


def mark_kernel(*refs):
    refs[-1][...] = jnp.zeros(refs[-1].shape, F32)


def mark(name, after, kept):
    return pl.pallas_call(
        mark_kernel,
        out_shape=jax.ShapeDtypeStruct((8, 128), F32),
        in_specs=[UNREAD] * len(after) + [WHOLE] * len(kept),
        out_specs=WHOLE,
        compiler_params=params(),
        cost_estimate=cost(LONG),
        name=name,
    )(*after, *kept)


def hold_kernel(*refs):
    refs[-1][...] = refs[0][...]


def hold(name, value, after):
    return pl.pallas_call(
        hold_kernel,
        out_shape=jax.ShapeDtypeStruct(value.shape, value.dtype),
        in_specs=[WHOLE] + [UNREAD] * len(after),
        out_specs=WHOLE,
        compiler_params=params(),
        cost_estimate=cost(LONG),
        name=name,
    )(value, *after)


def join_kernel(pairs, counts, *refs):
    outs = refs[-pairs:]
    rows = outs[0].shape[1]
    start = 0
    low = 0
    for count in counts:
        keep_ref, *came_refs = refs[start : start + 1 + count]
        start += 1 + count
        came = jnp.concatenate([ref[...].astype(F32) for ref in came_refs], axis=1)
        part = slice(low, low + keep_ref.shape[2])
        low += keep_ref.shape[2]
        outs[0][:, :, part] = keep_ref[:, :rows] + came[:, :rows]
        for dp in range(1, pairs):
            block = slice(dp * rows, (dp + 1) * rows)
            outs[dp][:, :, part] = (keep_ref[:, block] + came[:, block]).astype(BF16)


def join(pairs, name, sums, after):
    width = sum(item[0].shape[2] for item in sums)
    shape = (2, sums[0][0].shape[1] // pairs, width)
    counts = [len(item) - 1 for item in sums]
    flat = [part for item in sums for part in item]
    return pl.pallas_call(
        functools.partial(join_kernel, pairs, counts),
        out_shape=[jax.ShapeDtypeStruct(shape, F32)]
        + [jax.ShapeDtypeStruct(shape, BF16)] * (pairs - 1),
        in_specs=[WHOLE] * len(flat) + [UNREAD] * len(after),
        out_specs=[WHOLE] * pairs,
        compiler_params=params(),
        cost_estimate=cost(),
        name=name,
    )(*flat, *after)


def act_kernel(count, own_ref, *refs):
    sums = own_ref[...]
    for ref in refs[:count]:
        sums = sums + ref[...].astype(F32)
    gate = sums[0]
    refs[-1][...] = (gate / (1.0 + jnp.exp(-gate)) * sums[1]).astype(BF16)


def activate(name, own, arrived, after, flops=10**6):
    return pl.pallas_call(
        functools.partial(act_kernel, len(arrived)),
        out_shape=jax.ShapeDtypeStruct(own.shape[1:], BF16),
        in_specs=[WHOLE] * (1 + len(arrived)) + [UNREAD] * len(after),
        out_specs=WHOLE,
        compiler_params=params(),
        cost_estimate=cost(flops),
        name=name,
    )(own, *arrived, *after)


def served_kernel(batches, rows, counts, *refs):
    out_ref, mark_ref = refs[-2:]
    mark_ref[...] = jnp.zeros(mark_ref.shape, F32)
    turned = lax.axis_index("ffn") * rows
    seqs = batches * rows
    groups = []
    start = 0
    for count in counts:
        parts = [ref[...].astype(F32) for ref in refs[start : start + count]]
        groups.append(jnp.concatenate(parts, axis=1))
        start += count
    for micro in range(batches):
        low = micro * rows
        mine = [p[s + low : s + low + rows] for p in groups for s in range(0, p.shape[0], seqs)]
        mine = jnp.concatenate(mine, axis=0)
        out_ref[micro, 0] = pltpu.roll(mine, turned, 0).astype(BF16)


def serve(batches, rows, hidden):
    flat = [part for group in hidden for part in group]
    width = sum(part.shape[1] for part in hidden[0])
    total_rows = sum(group[0].shape[0] for group in hidden)
    return pl.pallas_call(
        functools.partial(served_kernel, batches, rows, [len(group) for group in hidden]),
        out_shape=[
            jax.ShapeDtypeStruct((batches, 1, total_rows // batches, width), BF16),
            jax.ShapeDtypeStruct((8, 128), F32),
        ],
        in_specs=[WHOLE] * len(flat),
        out_specs=[WHOLE] * 2,
        compiler_params=params(),
        cost_estimate=cost(LONG),
        name="serve",
    )(*flat)


def down_kernel(cols, batches, rows, sizes, parts, skip, table_ref, weight_ref, *refs):
    pairs, reps = cols
    columns = pairs * reps
    count = columns * sum(parts)
    held = []
    start = 0
    for part_count in parts:
        wide = []
        for _ in range(part_count):
            wide.append(jnp.concatenate([ref[...] for ref in refs[start : start + columns]], axis=0))
            start += columns
        held.append(jnp.concatenate(wide, axis=1))
    held = jnp.concatenate(held, axis=0)
    share_refs = refs[count + skip : -1]
    sums_ref = refs[-1]
    depth = weight_ref.shape[1]
    tile = math.gcd(depth, 256)
    for low in range(0, depth, tile):
        part = slice(low, low + tile)
        sums_ref[:, part] = jnp.dot(held, weight_ref[:, part], preferred_element_type=F32)
    seqs = batches * rows
    row = lax.broadcasted_iota(jnp.int32, (seqs, depth), 0)
    places = []
    for index in range(columns):
        held_at = []
        for micro in range(batches):
            column = table_ref[micro, place_of(index, cols)]
            to_pair = lax.rem(column // reps - lax.axis_index("pair") + pairs, pairs)
            to_rep = lax.rem(lax.rem(column, reps) - lax.axis_index("rep") + reps, reps)
            held_at.append(to_rep * pairs + to_pair)
        places.append(held_at)
    count = sum(sizes) // seqs
    mine_refs, peer_refs = share_refs[:count], share_refs[count : count + reps - 1]
    other_refs = share_refs[count + reps - 1 :]
    first = 0
    shift = 0
    for size in sizes:
        for inner in range(size // seqs):
            blocks = []
            for held_at in places:
                value = None
                for micro, place in enumerate(held_at):
                    base = pl.multiple_of(first + place * size + inner * seqs, seqs)
                    found = sums_ref[pl.ds(base, seqs), :]
                    value = jnp.where(row >= micro * rows, found, value) if micro else found
                blocks.append(value)
            mine_refs[shift][...] = blocks[0].astype(BF16)
            for dr in range(1, reps):
                peer_refs[dr - 1][shift] = blocks[dr * pairs].astype(BF16)
            other = [blocks[dr * pairs + dp] for dp in range(1, pairs) for dr in range(reps)]
            other_refs[shift][...] = jnp.concatenate(other, axis=0).astype(BF16)
            shift += 1
        first += columns * size


def down(cols, name, batches, rows, table, blocks, weight, after):
    pairs, reps = cols
    depth = weight.shape[1]
    seqs = batches * rows
    sizes = [group[0][0].shape[0] for group in blocks]
    parts = [len(group) for group in blocks]
    shifts = sum(sizes) // seqs
    flat = [item for group in blocks for block in group for item in block]
    mine = jax.ShapeDtypeStruct((seqs, depth), BF16)
    peer = jax.ShapeDtypeStruct((shifts, seqs, depth), BF16)
    other = jax.ShapeDtypeStruct(((pairs - 1) * reps * seqs, depth), BF16)
    out = pl.pallas_call(
        functools.partial(down_kernel, cols, batches, rows, sizes, parts, len(after)),
        out_shape=[mine] * shifts + [peer] * (reps - 1) + [other] * shifts,
        in_specs=[TABLE] + [WHOLE] * (1 + len(flat)) + [UNREAD] * len(after),
        out_specs=[WHOLE] * (2 * shifts + reps - 1),
        scratch_shapes=[pltpu.VMEM((sum(sizes) * pairs * reps, depth), F32)],
        compiler_params=params(8),
        cost_estimate=cost(LONG),
        name=name,
    )(table, weight, *flat, *after)
    return out[:shifts], out[shifts : shifts + reps - 1], out[shifts + reps - 1 :]


def merge_kernel(shifts, reps, *refs):
    out_refs = refs[-shifts:]
    for shift, out_ref in enumerate(out_refs):
        out_ref[0] = refs[shift][...]
        for dr in range(1, reps):
            out_ref[dr] = refs[shifts + dr - 1][shift]


def merge(mine, peers, after):
    shifts, reps = len(mine), len(peers) + 1
    return pl.pallas_call(
        functools.partial(merge_kernel, shifts, reps),
        out_shape=[jax.ShapeDtypeStruct((reps, *mine[0].shape), BF16)] * shifts,
        in_specs=[WHOLE] * (shifts + reps - 1) + [UNREAD] * len(after),
        out_specs=[WHOLE] * shifts,
        compiler_params=params(),
        cost_estimate=cost(),
        name="merge",
    )(*mine, *peers, *after)


def total_kernel(count, outs, *refs):
    sums = refs[0][...].astype(F32)
    for ref in refs[1:count]:
        sums = sums + ref[...].astype(F32)
    if sums.ndim == 2:
        sums = sums.reshape(outs, sums.shape[0] // outs, sums.shape[1])
    for index, out_ref in enumerate(refs[-outs:]):
        out_ref[...] = sums[index].astype(BF16)


def total(name, seqs, parts, after):
    outs = parts[0].size // parts[0].shape[-1] // seqs
    return pl.pallas_call(
        functools.partial(total_kernel, len(parts), outs),
        out_shape=[jax.ShapeDtypeStruct((seqs, parts[0].shape[-1]), BF16)] * outs,
        in_specs=[WHOLE] * len(parts) + [UNREAD] * len(after),
        out_specs=[WHOLE] * outs,
        compiler_params=params(),
        cost_estimate=cost(LONG),
        name=name,
    )(*parts, *after)


def finish_kernel(cols, pieces, stream_ref, *refs):
    out_ref = refs[-1]
    batches, _, rows, depth = out_ref.shape
    width = depth // (cols[0] * cols[1])
    start = 0
    for index, count in enumerate(pieces):
        column = place_of(index, cols, -1)
        for piece in range(count):
            ref = refs[start + piece]
            low = column * width + piece * (width // count)
            own = pl.ds(pl.multiple_of(low, width // count), width // count)
            sums = stream_ref[:, own] + ref[...].astype(F32)
            for micro in range(batches):
                out_ref[micro, 0, :, own] = sums[micro * rows : (micro + 1) * rows]
        start += count


def finish(cols, batches, stream, changes):
    seqs, depth = stream.shape
    flat = [part for parts in changes for part in parts]
    return pl.pallas_call(
        functools.partial(finish_kernel, cols, [len(parts) for parts in changes]),
        out_shape=jax.ShapeDtypeStruct((batches, 1, seqs // batches, depth), F32),
        in_specs=[WHOLE] * (1 + len(flat)),
        out_specs=WHOLE,
        compiler_params=params(),
        cost_estimate=cost(),
        name="finish",
    )(stream, *flat)


def to_column(cols, value, dr, dp):
    pairs, reps = cols
    route = [
        (p * reps + r, (p + dp) % pairs * reps + (r + dr) % reps)
        for p in range(pairs)
        for r in range(reps)
    ]
    return lax.ppermute(value, ("pair", "rep"), route)


def turn(value, ffn, shift):
    return lax.ppermute(value, "ffn", [(i, (i + shift) % ffn) for i in range(ffn)])


def per_device(
    cols,
    ffn,
    residual,
    query,
    key_cache,
    value_cache,
    cache_len,
    partner_table,
    norm_gain,
    gate_weight,
    up_weight,
    down_weight,
):
    pairs, reps = cols
    batches, _, rows, _ = query.shape
    stream, *normed = attend(
        cols, cache_len, query, key_cache, value_cache, residual, norm_gain
    )
    half = ffn // 2

    def spread(parts):
        return [to_column(cols, part, 0, dp + 1) for dp, part in enumerate(parts)]

    def swap(sums):
        return [sums[0], *[to_column(cols, part, 1, 0) for part in sums[1:]]]

    def collect(hidden):
        block = [hidden] + [to_column(cols, hidden, 0, pairs - dp) for dp in range(1, pairs)]
        return block + [to_column(cols, item, 1, 0) for item in block]

    mine = pack(cols, batches, partner_table, [
        to_column(cols, piece, *divmod(index, pairs)) if index else piece
        for index, piece in enumerate(normed)
    ])
    packs = [mine] + [turn(mine, ffn, -s) for s in range(1, ffn)]
    near, far = packs[:half], packs[half:]
    weights = (gate_weight, up_weight)
    units = gate_weight.shape[1] // 128
    edge = units // 2 * 128
    spans = ((0, edge), (edge, units * 128))
    held, *first = gate_up(cols, "gate_up_near_0", near, weights, spans[0], [], 1, LONG)
    second = gate_up(cols, "gate_up_near_1", [held], weights, spans[1], [], 1, LONG)
    here = mark("far_here", far, [])
    near_own, *near_sent = join(pairs, "join_near", [swap(first), swap(second)], [here])
    near_came = spread(near_sent)
    held, *first = gate_up(cols, "gate_up_far_0", far, weights, spans[0], [near_own], pairs, LONG)
    second = gate_up(cols, "gate_up_far_1", [held], weights, spans[1], [], pairs, 10**6)
    first_own, *first_sent = join(pairs, "join_far_0", [swap(first)], [])
    first_came = spread(first_sent)
    near_hidden = activate("activate_near", near_own, near_came, [first_own], LONG)
    second_own, *second_sent = join(pairs, "join_far_1", [swap(second)], [])
    second_came = spread(second_sent)
    first_hidden = activate("activate_far_0", first_own, first_came, [])
    second_hidden = activate("activate_far_1", second_own, second_came, [])
    hiddens = [[near_hidden], [first_hidden, second_hidden]]
    blocks = [[collect(part) for part in group] for group in hiddens]
    served, placed = serve(batches, rows, hiddens)
    mine, peers, other = down(cols, "down", batches, rows, partner_table, blocks, down_weight, [])
    other = [other[0]] + [turn(other[s], ffn, s) for s in sorted(range(1, ffn), key=lambda s: [2, 1, 3].index(s) if s < 4 else s)]
    same = merge(
        mine, [to_column(cols, peer, dr + 1, 0) for dr, peer in enumerate(peers)], [placed]
    )
    same = [same[0]] + [turn(same[s], ffn, s) for s in range(1, ffn)]
    other = total("total_other", batches * rows, other, [same[0]])
    same = total("total_same", batches * rows, same, other[:1])
    changes = []
    for dr in range(reps):
        changes.append([same[dr]])
        for dp in range(1, pairs):
            changes.append([to_column(cols, other[(dp - 1) * reps + dr], dr, dp)])
    updated = finish(cols, batches, stream, changes)
    return (updated, served)


def solution(mesh):
    sizes = dict(mesh.shape)
    cols = (sizes["pair"], sizes["rep"])
    rows = P(None, ("parts", "pair", "rep"), "ffn", None)
    caches = P(None, ("parts", "pair", "rep"), "ffn", None, None)
    placed = (
        rows,
        rows,
        caches,
        caches,
        P(None, ("parts", "pair", "rep"), "ffn"),
        P("parts", None),
        P(),
        P(("pair", "rep"), "ffn"),
        P(("pair", "rep"), "ffn"),
        P("ffn", ("pair", "rep")),
    )
    return jax.shard_map(
        functools.partial(per_device, cols, sizes["ffn"]),
        mesh=mesh,
        in_specs=placed,
        out_specs=(rows, P(None, ("parts", "pair", "rep"), None, "ffn")),
        check_vma=False,
    )
```
